32 devices in a mesh: dap: 16 (over z, y, x), rep: 2 (over core).
Axes of the slice: x: 2, y: 2, z: 4, core: 2. Of those that a mesh axis runs over, the one named last changes fastest.
Arguments:
- pair: bfloat16 [256, 128, 128], P(('rep', 'dap')), parts along dimension 0, may hold values from -6 to 6
- w_proj: bfloat16 [128, 512], replicated, may hold values from -0.5 to 0.5
- w_gate_out: bfloat16 [128, 128], replicated, may hold values from -0.5 to 0.5
- w_out: bfloat16 [128, 128], replicated, may hold values from -0.5 to 0.5
- w_qkvg: bfloat16 [128, 512], replicated, may hold values from -0.5 to 0.5
- w_bias: bfloat16 [128, 4], replicated
- w_att_out: bfloat16 [128, 128], replicated, may hold values from -0.5 to 0.5
- length: int32 [2], P('rep'), parts along dimension 0, may hold values from 64 to 128
Outputs:
- pair_out: bfloat16 [256, 128, 128], P('rep', 'dap'), parts along dimension 0
The draws below stay inside these ranges and needn't reach their ends.
There are 2 independent parts, one for each index of `rep`. The reference program is written for one: setup_inputs(seed, part) draws one part's arguments, and reference() takes and returns one part's arrays. A program takes and returns all parts, laid end to end along the dimension named above; an argument that names none is the same for every part. Nothing has to cross between parts.
All inputs are finite; a program needn't handle non-finite values.
Results may differ from the reference program's by a relative error of at most 0.017.
The reference program's roundings to bfloat16 on the way (of `normed`, `product_norm`, `pair_mid`, `normed_mid`, `bias`, `weights` and `attended`) count: a program that leaves them out, or rounds other values in their place, can miss the bound.
Values may be sent and summed in bfloat16 or wider, within the bound.
No kernel may reach another device: no remote copies, remote signals or barrier semaphores. Data moves between devices by JAX's collectives and lax.ppermute only.
A program may use at most 192 MiB of HBM per device.

```python
import jax
import jax.numpy as jnp
from jax import lax

C = 128
CH = 128
H = 4
DH = 32
N = 128


def draw_length(key, part):
    key = jax.random.fold_in(key, 11)
    drawn = jax.random.randint(key, (1,), N // 2, N, dtype=jnp.int32)
    return jnp.where(part % 2 == 1, jnp.full((1,), N, dtype=jnp.int32), drawn).astype(jnp.int32)


def draw_w_bias(key, part):
    key = jax.random.fold_in(key, 23)
    base = jax.random.normal(key, (C, H), dtype=jnp.float32)
    factor = C ** (-0.5)
    return (base * factor).astype(jnp.bfloat16)


def level_of(own_key, extent, shards, low, largest):
    def one(dim, shards_of):
        heights = jax.random.uniform(jax.random.fold_in(jax.random.fold_in(own_key, 6), dim), (shards_of,), jnp.float32, low / len(shards), largest / len(shards))
        return jnp.repeat(jnp.exp(heights), extent[dim] // shards_of).reshape((-1,) + (1,) * (len(extent) - dim - 1))

    gain = one(*shards[0])
    for cut in shards[1:]:
        gain = gain * one(*cut)
    return gain


def gaussian(key, extent, scale, reach, cuts=(), held_as=jnp.bfloat16):
    array = jax.random.normal(key, extent, jnp.float32) * scale
    if len(cuts) > 0:
        array = level_of(key, extent, cuts, -0.22, 0.18) * array
    return jnp.clip(array, min=-reach, max=reach).astype(held_as)


def setup_inputs(seed: int = 0, part: int = 0) -> dict:
    key_list = jax.random.split(jax.random.key(seed), 9)
    own_keys = jax.random.split(jax.random.fold_in(key_list[8], part), 9)
    return {
        "pair": gaussian(own_keys[0], (N, N, C), 1.0, 6.0, ((0, 16),)),
        "w_proj": gaussian(key_list[1], (C, 4 * CH), C ** -0.5, 0.5),
        "w_gate_out": gaussian(key_list[2], (C, C), C ** -0.5, 0.5),
        "w_out": gaussian(key_list[3], (CH, C), CH ** -0.5, 0.5),
        "w_qkvg": gaussian(key_list[4], (C, 4 * H * DH), C ** -0.5, 0.5),
        "w_bias": draw_w_bias(jax.random.fold_in(key_list[8], 71), part),
        "w_att_out": gaussian(key_list[6], (H * DH, C), (H * DH) ** -0.5, 0.5),
        "length": draw_length(jax.random.fold_in(jax.random.fold_in(key_list[8], part), 71), part),
    }


def layer_norm(x, axis):
    mean = lax.optimization_barrier(jnp.mean(x, axis=axis, keepdims=True))
    centered = x - mean
    spread = lax.optimization_barrier(jnp.mean(centered * centered, axis=axis, keepdims=True))
    return centered * lax.rsqrt(spread + 1e-05)

def reference(pair, w_proj, w_gate_out, w_out, w_qkvg, w_bias, w_att_out, length):
    positions = jnp.arange(N, dtype=jnp.int32)
    valid = (positions < length[0]).astype(jnp.float32)
    normed = layer_norm(pair.astype(jnp.float32), 2).astype(jnp.bfloat16)
    normed_wide = normed.astype(jnp.float32)
    projected = jnp.einsum('rnc,ce->ern', normed_wide, w_proj.astype(jnp.float32))
    pair_mask = valid[:, None] * valid[None, :]
    left = (jax.nn.sigmoid(projected[CH:2 * CH]) * projected[:CH] * pair_mask[None]).astype(jnp.bfloat16)
    right = (jax.nn.sigmoid(projected[3 * CH:]) * projected[2 * CH:3 * CH] * pair_mask[None]).astype(jnp.bfloat16)
    product = jnp.einsum('cik,cjk->cij', left.astype(jnp.float32), right.astype(jnp.float32), precision=lax.Precision.HIGHEST)
    product_norm = layer_norm(product, 0).astype(jnp.bfloat16)
    update = jnp.einsum('cij,cd->ijd', product_norm.astype(jnp.float32), w_out.astype(jnp.float32))
    gate_out = jax.nn.sigmoid(jnp.einsum('ijc,cd->ijd', normed_wide, w_gate_out.astype(jnp.float32)))
    pair_mid = (pair.astype(jnp.float32) + gate_out * update).astype(jnp.bfloat16)
    normed_mid = layer_norm(pair_mid.astype(jnp.float32), 2).astype(jnp.bfloat16).astype(jnp.float32)
    bias = jnp.einsum('kic,ch->hki', normed_mid, w_bias.astype(jnp.float32)).astype(jnp.bfloat16)
    bias_turned = jnp.transpose(bias, (0, 2, 1)).astype(jnp.float32)
    width = H * DH
    mixed = jnp.einsum('ijc,ce->ije', normed_mid, w_qkvg.astype(jnp.float32))
    queries = mixed[..., :width].astype(jnp.bfloat16).reshape(N, N, H, DH)
    keys_all = mixed[..., width:2 * width].astype(jnp.bfloat16).reshape(N, N, H, DH)
    values_all = mixed[..., 2 * width:3 * width].astype(jnp.bfloat16).reshape(N, N, H, DH)
    gate = jax.nn.sigmoid(mixed[..., 3 * width:]).reshape(N, N, H, DH)
    scale = DH ** (-0.5)

    def one_column(column):
        query_col = lax.dynamic_index_in_dim(queries, column, 1, False).astype(jnp.float32)
        key_col = lax.dynamic_index_in_dim(keys_all, column, 1, False).astype(jnp.float32)
        value_col = lax.dynamic_index_in_dim(values_all, column, 1, False).astype(jnp.float32)
        gate_col = lax.dynamic_index_in_dim(gate, column, 1, False)
        score = jnp.einsum('ihd,khd->hik', query_col, key_col) * scale + bias_turned
        score = jnp.where(valid[None, None, :] > 0, score, -1000000000.0)
        top = lax.optimization_barrier(jnp.max(score, axis=2, keepdims=True))
        expo = jnp.exp(score - top)
        weights = (expo / lax.optimization_barrier(jnp.sum(expo, axis=2, keepdims=True))).astype(jnp.bfloat16)
        output = jnp.einsum('hik,khd->ihd', weights.astype(jnp.float32), value_col)
        return (gate_col * output).astype(jnp.bfloat16).reshape(N, width)
    attended = lax.map(one_column, jnp.arange(N, dtype=jnp.int32))
    attended = jnp.transpose(attended, (1, 0, 2)).astype(jnp.float32)
    result = pair_mid.astype(jnp.float32) + jnp.einsum('ije,ec->ijc', attended, w_att_out.astype(jnp.float32))
    return result.astype(jnp.bfloat16)
```

```python
import jax
import jax.numpy as jnp
from jax import lax
from jax.sharding import PartitionSpec as P


def layer_norm(x, axis):
    mean = jnp.mean(x, axis=axis, keepdims=True)
    centered = x - mean
    spread = jnp.mean(centered * centered, axis=axis, keepdims=True)
    return centered * lax.rsqrt(spread + 1e-05)


def exchange(x):
    return lax.all_to_all(x, "dap", split_axis=0, concat_axis=0, tiled=True)


def matmul(spec, a, b):
    return jnp.einsum(spec, a, b, preferred_element_type=jnp.float32)


def body(pair, w_proj, w_gate_out, w_out, w_qkvg, w_bias, w_att_out, length):
    row_count, full_count, channels = pair.shape
    hidden = w_out.shape[0]
    device_count = full_count // row_count
    share = hidden // device_count
    my_index = lax.axis_index("dap")
    positions = jnp.arange(full_count, dtype=jnp.int32)
    valid_keys = (positions < length[0]).astype(jnp.float32)
    row_valid = lax.dynamic_slice_in_dim(valid_keys, my_index * row_count, row_count)

    normed = layer_norm(pair.astype(jnp.float32), 2).astype(jnp.bfloat16)
    projected = matmul("rnc,ce->ern", normed, w_proj)
    pair_mask = row_valid[:, None] * valid_keys[None, :]
    left = jax.nn.sigmoid(projected[hidden : 2 * hidden]) * projected[:hidden] * pair_mask
    right = jax.nn.sigmoid(projected[3 * hidden :]) * projected[2 * hidden : 3 * hidden] * pair_mask
    blocks = (device_count, share * row_count, full_count)
    left = left.astype(jnp.bfloat16).reshape(blocks)
    right = right.astype(jnp.bfloat16).reshape(blocks)
    columns = jnp.transpose(
        pair.reshape(row_count, device_count, row_count, channels), (1, 0, 2, 3)
    )
    cut = share * row_count * full_count
    sent = jnp.concatenate(
        [
            left.reshape(device_count, cut),
            right.reshape(device_count, cut),
            columns.reshape(device_count, row_count * row_count * channels),
        ],
        axis=1,
    )
    came = exchange(sent.reshape(device_count, -1, channels)).reshape(device_count, -1)
    rows = (device_count, share, row_count, full_count)
    left = jnp.transpose(came[:, :cut].reshape(rows), (1, 0, 2, 3))
    right = jnp.transpose(came[:, cut : 2 * cut].reshape(rows), (1, 0, 2, 3))
    columns = came[:, 2 * cut :].reshape(full_count, row_count, channels)

    square = (share, full_count, full_count)
    product = matmul("cjk,cik->cji", right.reshape(square), left.reshape(square))
    product = product.astype(jnp.bfloat16).reshape(share, device_count, row_count, full_count)
    product = exchange(jnp.transpose(product, (1, 0, 2, 3)))
    product = product.reshape(hidden, row_count, full_count)
    product_norm = layer_norm(product.astype(jnp.float32), 0).astype(jnp.bfloat16)
    update = matmul("cji,cd->ijd", product_norm, w_out)
    normed = layer_norm(columns.astype(jnp.float32), 2).astype(jnp.bfloat16)
    gate_out = jax.nn.sigmoid(matmul("ijc,cd->ijd", normed, w_gate_out))
    columns = (columns.astype(jnp.float32) + gate_out * update).astype(jnp.bfloat16)

    normed_mid = layer_norm(columns.astype(jnp.float32), 2).astype(jnp.bfloat16)
    heads = w_bias.shape[1]
    width = w_att_out.shape[0]
    head_size = width // heads
    bias = matmul("kic,ch->hik", normed_mid, w_bias).astype(jnp.bfloat16)
    bias = exchange(jnp.broadcast_to(bias[None], (device_count,) + bias.shape))
    bias = jnp.transpose(bias, (1, 0, 2, 3)).reshape(heads, full_count, full_count)

    mixed = matmul("ijc,ce->ije", normed_mid, w_qkvg)
    per_head = (full_count, row_count, heads, head_size)
    queries = mixed[..., :width].astype(jnp.bfloat16).reshape(per_head)
    keys = mixed[..., width : 2 * width].astype(jnp.bfloat16).reshape(per_head)
    values = mixed[..., 2 * width : 3 * width].astype(jnp.bfloat16).reshape(per_head)
    gate = jax.nn.sigmoid(mixed[..., 3 * width :])
    score = matmul("ijhd,kjhd->jhik", queries, keys) * head_size ** (-0.5)
    score = score + bias.astype(jnp.float32)[None]
    score = jnp.where(valid_keys > 0, score, -1000000000.0)
    top = jnp.max(score, axis=3, keepdims=True)
    expo = jnp.exp(score - top)
    weights = (expo / jnp.sum(expo, axis=3, keepdims=True)).astype(jnp.bfloat16)
    output = matmul("jhik,kjhd->ijhd", weights, values)
    attended = (gate * output.reshape(full_count, row_count, width)).astype(jnp.bfloat16)
    result = columns.astype(jnp.float32) + matmul("ije,ec->ijc", attended, w_att_out)
    return result.astype(jnp.bfloat16)


def solution(mesh):
    placed = (P(("rep", "dap"), None, None), P(), P(), P(), P(), P(), P(), P("rep"))
    return jax.shard_map(
        body, mesh=mesh, in_specs=placed, out_specs=P("rep", "dap", None), check_vma=False
    )
```

```python
import functools

import jax
import jax.numpy as jnp
from jax import lax
from jax.experimental import pallas as pl
from jax.experimental.pallas import tpu as pltpu
from jax.sharding import PartitionSpec as P

VMEM = pl.BlockSpec(memory_space=pltpu.VMEM)
SMEM = pl.BlockSpec(memory_space=pltpu.SMEM)
BF16, F32 = jnp.bfloat16, jnp.float32


def dot(a, b, over_a, over_b):
    return lax.dot_general(a, b, (((over_a,), (over_b,)), ((), ())), preferred_element_type=F32)


def sigmoid(x):
    return 0.5 * jnp.tanh(0.5 * x) + 0.5


def layer_norm(x, axis):
    mean = jnp.mean(x, axis=axis, keepdims=True)
    centered = x - mean
    spread = jnp.mean(centered * centered, axis=axis, keepdims=True)
    return centered * lax.rsqrt(spread + 1e-05)


def interleave(a, b, blocks):
    split = (blocks, a.shape[0] // blocks, a.shape[1])
    return jnp.concatenate([a.reshape(split), b.reshape(split)], axis=1).astype(BF16)


def project_kernel(length_ref, pair_ref, w_ref, out_ref):
    rows, count, channels = pair_ref.shape
    blocks = out_ref.shape[0]
    hidden = w_ref.shape[1] // 4
    first_row = lax.axis_index("dap") * rows
    length = length_ref[0]
    key_valid = jnp.where(lax.broadcasted_iota(jnp.int32, (1, count), 1) < length, 1.0, 0.0)
    w_turned = w_ref[...].T
    for r in range(rows):
        x = pair_ref[r].astype(F32)
        normed = layer_norm(x, 1).astype(BF16)
        projected = dot(w_turned, normed, 1, 1)
        mask = key_valid * jnp.where(first_row + r < length, 1.0, 0.0)
        left = sigmoid(projected[hidden : 2 * hidden]) * projected[:hidden] * mask
        right = sigmoid(projected[3 * hidden :]) * projected[2 * hidden : 3 * hidden] * mask
        out_ref[:, 16 * r : 16 * r + 16, :] = interleave(left, right, blocks)
        if r % 2 == 1:
            start = 16 * rows + 8 * (r - 1)
            out_ref[:, start : start + 16, :] = interleave(before, x, blocks)
        before = x


def product_kernel(came_ref, out_ref, wide_ref):
    blocks, per_block, count = came_ref.shape
    for p in range(blocks):
        wide_ref[p * per_block : (p + 1) * per_block, :] = came_ref[p].astype(F32)

    def product(c):
        left = wide_ref[pl.ds(c, count, stride=16), :].astype(BF16)
        right = wide_ref[pl.ds(8 + c, count, stride=16), :].astype(BF16)
        return dot(right, left, 1, 1)

    for c in range(0, 8, 2):
        out_ref[:, 8 * c : 8 * c + 16, :] = interleave(product(c), product(c + 1), blocks)


def gate_kernel(came_ref, w_ref, gate_ref, columns_ref, wide_ref):
    blocks, per_block, channels = came_ref.shape
    count, columns = gate_ref.shape[1], gate_ref.shape[0]
    for p in range(blocks):
        wide_ref[p * per_block : (p + 1) * per_block, :] = came_ref[p].astype(F32)
    w = w_ref[...]
    for j in range(columns):
        x = wide_ref[pl.ds(j, count, stride=columns), :]
        columns_ref[j] = x.astype(BF16)
        gate_ref[j] = sigmoid(dot(layer_norm(x, 1).astype(BF16), w, 1, 0))


def middle_kernel(came_ref, gate_ref, columns_ref, w_out_ref, w_bias_ref, bias_ref, normed_ref, mid_ref, wide_ref):
    columns, count, channels = mid_ref.shape
    x = came_ref[...].astype(F32).reshape(-1, columns, count)
    hidden = x.shape[0]
    wide_ref[...] = layer_norm(x, 0).reshape(hidden * columns, count)
    w_out = w_out_ref[...]
    w_bias = w_bias_ref[...]
    own = lax.broadcasted_iota(jnp.int32, w_bias.shape, 0) % columns
    total = jnp.zeros((w_bias.shape[0], count), F32)
    for j in range(columns):
        product = wide_ref[pl.ds(j, hidden, stride=columns), :].astype(BF16)
        update = dot(product, w_out, 0, 0)
        mid = (columns_ref[j].astype(F32) + gate_ref[j] * update).astype(BF16)
        mid_ref[j] = mid
        normed = layer_norm(mid.astype(F32), 1).astype(BF16)
        normed_ref[j] = normed
        total += dot(jnp.where(own == j, w_bias, 0.0).astype(BF16), normed, 1, 1)
    bias_ref[...] = jnp.broadcast_to(total.astype(BF16)[None], bias_ref.shape)


def heads_kernel(heads, normed_ref, w_ref, q_ref, k_ref, v_ref, g_ref):
    columns, count, channels = normed_ref.shape
    width = q_ref.shape[2]
    size = width // heads
    w = w_ref[...]
    w_turned = w[:, 2 * width :].T
    lane = lax.broadcasted_iota(jnp.int32, (count, width), 1) // size
    row = lax.broadcasted_iota(jnp.int32, (width, count), 0) // size
    for j in range(columns):
        normed = normed_ref[j]
        qk = dot(normed, w[:, : 2 * width], 1, 0)
        q_ref[j] = qk[:, :width].astype(BF16)
        vg = dot(w_turned, normed, 1, 1)
        g_ref[j] = sigmoid(vg[width:])
        for h in range(heads):
            k_ref[j, h * count : (h + 1) * count, :] = jnp.where(lane == h, qk[:, width:], 0.0).astype(BF16)
            v_ref[j, :, h * count : (h + 1) * count] = jnp.where(row == h, vg[:width], 0.0).astype(BF16)


def attention_kernel(heads, length_ref, bias_ref, q_ref, k_ref, v_ref, g_ref, mid_ref, w_ref, out_ref, wide_ref):
    columns, count, width = q_ref.shape
    size = width // heads
    blocks = bias_ref.shape[0]
    invalid = lax.broadcasted_iota(jnp.int32, (count, count), 0) >= length_ref[0]
    arrived = bias_ref[...].astype(F32).reshape(blocks, heads, columns, count)
    bias = [arrived[:, h].reshape(count, count).T for h in range(heads)]
    w = w_ref[...]
    for j in range(columns):
        q = q_ref[j]
        parts = []
        for h in range(heads):
            score = dot(k_ref[j, h * count : (h + 1) * count, :], q, 1, 1) * size ** (-0.5) + bias[h]
            score = jnp.where(invalid, -1000000000.0, score)
            expo = jnp.exp(score - jnp.max(score, axis=0, keepdims=True))
            total = jnp.sum(expo, axis=0, keepdims=True)
            parts.append((expo * (1.0 / total)).astype(BF16))
        output = dot(v_ref[j], jnp.concatenate(parts, axis=0), 1, 0)
        attended = (g_ref[j] * output).astype(BF16)
        result = dot(attended, w, 0, 0) + mid_ref[j].astype(F32)
        wide_ref[pl.ds(j, count, stride=columns), :] = result
    out_ref[...] = wide_ref[...].reshape(count, columns, w.shape[1]).astype(BF16)


def call(kernel, outs, operands, specs=None, scratch=(), flops=0, grid=()):
    size = sum(a.size * a.dtype.itemsize for a in list(operands) + list(outs))
    return pl.pallas_call(
        kernel,
        grid=grid,
        out_shape=[jax.ShapeDtypeStruct(o.shape, o.dtype) for o in outs],
        in_specs=[VMEM] * len(operands) if specs is None else specs,
        out_specs=[VMEM] * len(outs),
        scratch_shapes=list(scratch),
        cost_estimate=pl.CostEstimate(flops=flops, bytes_accessed=size, transcendentals=0),
        compiler_params=pltpu.CompilerParams(vmem_limit_bytes=24 * 2**20),
    )(*operands)


def shape(dims, dtype):
    return jax.ShapeDtypeStruct(dims, dtype)


def exchange(x):
    return lax.all_to_all(x, "dap", split_axis=0, concat_axis=0, tiled=True)


def kernel_body(pair, w_proj, w_gate_out, w_out, w_qkvg, w_bias, w_att_out, length):
    rows, count, channels = pair.shape
    hidden = w_out.shape[0]
    blocks = count // rows
    heads, width = w_bias.shape[1], w_att_out.shape[0]
    square = (rows, count, channels)
    wide = pltpu.VMEM((rows * count, channels), F32)

    (sent,) = call(
        project_kernel,
        [shape((blocks, 24 * rows, count), BF16)],
        (length, pair, w_proj),
        [SMEM, VMEM, VMEM],
        flops=2 * pair.size * 4 * hidden,
    )
    came = exchange(sent)
    (product,) = call(
        product_kernel,
        [shape((blocks, 8 * rows, count), BF16)],
        (came,),
        [pl.BlockSpec((blocks, 16 * rows, count), lambda _: (0, 0, 0))],
        [pltpu.VMEM((blocks * 16 * rows, count), F32)],
        flops=2 * 8 * count**3,
        grid=(1,),
    )
    arrived = exchange(product)
    gate, columns = call(
        gate_kernel,
        [shape(square, F32), shape(square, BF16)],
        (came, w_gate_out),
        [pl.BlockSpec((blocks, 8 * rows, channels), lambda _: (0, 2, 0)), VMEM],
        [wide],
        flops=2 * pair.size * channels,
        grid=(1,),
    )
    w_rows = jnp.repeat(w_bias.T, rows, axis=0).astype(F32)
    bias, normed, mid = call(
        middle_kernel,
        [shape((blocks, heads * rows, count), BF16), shape(square, BF16), shape(square, BF16)],
        (arrived, gate, columns, w_out, w_rows),
        scratch=[wide],
        flops=2 * pair.size * channels,
    )
    bias = exchange(bias)
    q, k, v, g = call(
        functools.partial(heads_kernel, heads),
        [
            shape((rows, count, width), BF16),
            shape((rows, heads * count, width), BF16),
            shape((rows, width, heads * count), BF16),
            shape((rows, width, count), F32),
        ],
        (normed, w_qkvg),
        flops=2 * pair.size * 4 * width,
    )
    (out,) = call(
        functools.partial(attention_kernel, heads),
        [shape((count, rows, channels), BF16)],
        (length, bias, q, k, v, g, mid, w_att_out),
        [SMEM] + [VMEM] * 7,
        [wide],
        flops=2 * pair.size * count * 8,
    )
    return out


def matmul(spec, a, b):
    return jnp.einsum(spec, a, b, preferred_element_type=jnp.float32)


def whole_body(pair, w_proj, w_gate_out, w_out, w_qkvg, w_bias, w_att_out, length):
    row_count, full_count, channels = pair.shape
    hidden = w_out.shape[0]
    device_count = full_count // row_count
    share = hidden // device_count
    my_index = lax.axis_index("dap")
    positions = jnp.arange(full_count, dtype=jnp.int32)
    valid_keys = (positions < length[0]).astype(jnp.float32)
    row_valid = lax.dynamic_slice_in_dim(valid_keys, my_index * row_count, row_count)

    normed = layer_norm(pair.astype(jnp.float32), 2).astype(jnp.bfloat16)
    projected = matmul("rnc,ce->ern", normed, w_proj)
    pair_mask = row_valid[:, None] * valid_keys[None, :]
    left = jax.nn.sigmoid(projected[hidden : 2 * hidden]) * projected[:hidden] * pair_mask
    right = jax.nn.sigmoid(projected[3 * hidden :]) * projected[2 * hidden : 3 * hidden] * pair_mask
    blocks = (device_count, share * row_count, full_count)
    left = left.astype(jnp.bfloat16).reshape(blocks)
    right = right.astype(jnp.bfloat16).reshape(blocks)
    columns = jnp.transpose(
        pair.reshape(row_count, device_count, row_count, channels), (1, 0, 2, 3)
    )
    cut = share * row_count * full_count
    sent = jnp.concatenate(
        [
            left.reshape(device_count, cut),
            right.reshape(device_count, cut),
            columns.reshape(device_count, row_count * row_count * channels),
        ],
        axis=1,
    )
    came = exchange(sent.reshape(device_count, -1, channels)).reshape(device_count, -1)
    rows = (device_count, share, row_count, full_count)
    left = jnp.transpose(came[:, :cut].reshape(rows), (1, 0, 2, 3))
    right = jnp.transpose(came[:, cut : 2 * cut].reshape(rows), (1, 0, 2, 3))
    columns = came[:, 2 * cut :].reshape(full_count, row_count, channels)

    square = (share, full_count, full_count)
    product = matmul("cjk,cik->cji", right.reshape(square), left.reshape(square))
    product = product.astype(jnp.bfloat16).reshape(share, device_count, row_count, full_count)
    product = exchange(jnp.transpose(product, (1, 0, 2, 3)))
    product = product.reshape(hidden, row_count, full_count)
    product_norm = layer_norm(product.astype(jnp.float32), 0).astype(jnp.bfloat16)
    update = matmul("cji,cd->ijd", product_norm, w_out)
    normed = layer_norm(columns.astype(jnp.float32), 2).astype(jnp.bfloat16)
    gate_out = jax.nn.sigmoid(matmul("ijc,cd->ijd", normed, w_gate_out))
    columns = (columns.astype(jnp.float32) + gate_out * update).astype(jnp.bfloat16)

    normed_mid = layer_norm(columns.astype(jnp.float32), 2).astype(jnp.bfloat16)
    heads = w_bias.shape[1]
    width = w_att_out.shape[0]
    head_size = width // heads
    bias = matmul("kic,ch->hik", normed_mid, w_bias).astype(jnp.bfloat16)
    bias = exchange(jnp.broadcast_to(bias[None], (device_count,) + bias.shape))
    bias = jnp.transpose(bias, (1, 0, 2, 3)).reshape(heads, full_count, full_count)

    mixed = matmul("ijc,ce->ije", normed_mid, w_qkvg)
    per_head = (full_count, row_count, heads, head_size)
    queries = mixed[..., :width].astype(jnp.bfloat16).reshape(per_head)
    keys = mixed[..., width : 2 * width].astype(jnp.bfloat16).reshape(per_head)
    values = mixed[..., 2 * width : 3 * width].astype(jnp.bfloat16).reshape(per_head)
    gate = jax.nn.sigmoid(mixed[..., 3 * width :])
    score = matmul("ijhd,kjhd->jhik", queries, keys) * head_size ** (-0.5)
    score = score + bias.astype(jnp.float32)[None]
    score = jnp.where(valid_keys > 0, score, -1000000000.0)
    top = jnp.max(score, axis=3, keepdims=True)
    expo = jnp.exp(score - top)
    weights = (expo / jnp.sum(expo, axis=3, keepdims=True)).astype(jnp.bfloat16)
    output = matmul("jhik,kjhd->ijhd", weights, values)
    attended = (gate * output.reshape(full_count, row_count, width)).astype(jnp.bfloat16)
    result = columns.astype(jnp.float32) + matmul("ije,ec->ijc", attended, w_att_out)
    return result.astype(jnp.bfloat16)


def body(pair, w_proj, w_gate_out, w_out, w_qkvg, w_bias, w_att_out, length):
    rows, count, channels = pair.shape
    share = w_out.shape[0] * rows // count
    fits = share == rows == 8 and count == channels == w_att_out.shape[0] == 128
    chosen = kernel_body if fits else whole_body
    return chosen(pair, w_proj, w_gate_out, w_out, w_qkvg, w_bias, w_att_out, length)


def solution(mesh):
    placed = (P(("rep", "dap"), None, None), P(), P(), P(), P(), P(), P(), P("rep"))
    return jax.shard_map(
        body, mesh=mesh, in_specs=placed, out_specs=P("rep", "dap", None), check_vma=False
    )
```

```python
import functools

import jax
import jax.numpy as jnp
from jax import lax
from jax.experimental import pallas as pl
from jax.experimental.pallas import tpu as pltpu
from jax.sharding import PartitionSpec as P

VMEM = pl.BlockSpec(memory_space=pltpu.VMEM)
SMEM = pl.BlockSpec(memory_space=pltpu.SMEM)
HBM = pl.BlockSpec(memory_space=pltpu.HBM)
BF16, F32 = jnp.bfloat16, jnp.float32
LOG2E = 1.4426950408889634


def dot(a, b, over_a, over_b):
    return lax.dot_general(a, b, (((over_a,), (over_b,)), ((), ())), preferred_element_type=F32)


def sigmoid(x):
    return 0.5 * jnp.tanh(0.5 * x) + 0.5


def layer_norm(x, axis):
    mean = jnp.mean(x, axis=axis, keepdims=True)
    centered = x - mean
    spread = jnp.mean(centered * centered, axis=axis, keepdims=True)
    return centered * lax.rsqrt(spread + 1e-05)


def interleave(a, b, blocks):
    split = (blocks, a.shape[0] // blocks, a.shape[1])
    return jnp.concatenate([a.reshape(split), b.reshape(split)], axis=1).astype(BF16)


def project_kernel(length_ref, pair_hbm, w_hbm, out_ref, pair_ref, w_ref, sems):
    rows, count, channels = pair_ref.shape
    blocks = out_ref.shape[0]
    hidden = w_ref.shape[1] // 4
    copies = [pltpu.make_async_copy(w_hbm, w_ref, sems.at[0])]
    for r in range(0, rows, 2):
        part = pl.ds(r, 2)
        copies.append(pltpu.make_async_copy(pair_hbm.at[part], pair_ref.at[part], sems.at[1 + r // 2]))
    for copy in copies:
        copy.start()
    first_row = lax.axis_index("dap") * rows
    length = length_ref[0]
    key_valid = jnp.where(lax.broadcasted_iota(jnp.int32, (1, count), 1) < length, 1.0, 0.0)
    copies[0].wait()
    w_turned = w_ref[...].T
    for r in range(rows):
        if r % 2 == 0:
            copies[1 + r // 2].wait()
        x = pair_ref[r].astype(F32)
        normed = layer_norm(x, 1).astype(BF16)
        projected = dot(w_turned, normed, 1, 1)
        mask = key_valid * jnp.where(first_row + r < length, 1.0, 0.0)
        left = sigmoid(projected[hidden : 2 * hidden]) * projected[:hidden] * mask
        right = sigmoid(projected[3 * hidden :]) * projected[2 * hidden : 3 * hidden] * mask
        out_ref[:, 16 * r : 16 * r + 16, :] = interleave(left, right, blocks)
        if r % 2 == 1:
            start = 16 * rows + 8 * (r - 1)
            out_ref[:, start : start + 16, :] = interleave(before, x, blocks)
        before = x


def product_kernel(came_ref, out_ref, wide_ref):
    blocks, per_block, count = out_ref.shape[0], 2 * out_ref.shape[1], out_ref.shape[2]
    for p in range(blocks):
        wide_ref[p * per_block : (p + 1) * per_block, :] = came_ref[p, :per_block].astype(F32)

    def product(c):
        left = wide_ref[pl.ds(c, count, stride=16), :].astype(BF16)
        right = wide_ref[pl.ds(8 + c, count, stride=16), :].astype(BF16)
        return dot(right, left, 1, 1)

    for c in range(0, 8, 2):
        out_ref[:, 8 * c : 8 * c + 16, :] = interleave(product(c), product(c + 1), blocks)


def gate_kernel(came_ref, w_ref, gate_ref, columns_ref, wide_ref):
    columns, count = gate_ref.shape[0], gate_ref.shape[1]
    blocks, per_block = came_ref.shape[0], columns * columns
    for p in range(blocks):
        wide_ref[p * per_block : (p + 1) * per_block, :] = came_ref[p, 2 * per_block :].astype(F32)
    w = w_ref[...]
    for j in range(columns):
        x = wide_ref[pl.ds(j, count, stride=columns), :]
        columns_ref[j] = x.astype(BF16)
        gate_ref[j] = sigmoid(dot(layer_norm(x, 1).astype(BF16), w, 1, 0))


def middle_kernel(came_ref, gate_ref, columns_ref, w_out_ref, w_bias_ref, bias_ref, normed_ref, mid_ref, wide_ref):
    columns, count, channels = mid_ref.shape
    blocks, per_block, _ = came_ref.shape
    hidden = blocks * per_block // columns

    def load(p):
        return came_ref[p].astype(F32).reshape(per_block // columns, columns, count)

    mean = jnp.zeros((columns, count), F32)
    for p in range(blocks):
        mean += jnp.sum(load(p), axis=0)
    mean = mean * (1.0 / hidden)
    spread = jnp.zeros((columns, count), F32)
    for p in range(blocks):
        spread += jnp.sum(jnp.square(load(p) - mean), axis=0)
    scale = lax.rsqrt(spread * (1.0 / hidden) + 1e-05)
    for p in range(blocks):
        part = (load(p) - mean) * scale
        wide_ref[p * per_block : (p + 1) * per_block, :] = part.reshape(per_block, count)
    w_out = w_out_ref[...]
    for j in range(columns):
        product = wide_ref[pl.ds(j, hidden, stride=columns), :].astype(BF16)
        update = dot(product, w_out, 0, 0)
        mid_ref[j] = (columns_ref[j].astype(F32) + gate_ref[j] * update).astype(BF16)
    for j in range(columns):
        normed_ref[j] = layer_norm(mid_ref[j].astype(F32), 1).astype(BF16)
    w_bias = w_bias_ref[...]
    own = lax.broadcasted_iota(jnp.int32, w_bias.shape, 0) % columns
    total = jnp.zeros((w_bias.shape[0], count), F32)
    for j in range(columns):
        total += dot(jnp.where(own == j, w_bias, 0.0).astype(BF16), normed_ref[j], 1, 1)
    bias_ref[...] = jnp.broadcast_to(total.astype(BF16)[None], bias_ref.shape)


def heads_kernel(heads, length_ref, normed_ref, w_ref, score_ref, v_ref, gate_ref):
    columns, count, channels = normed_ref.shape
    width = gate_ref.shape[1]
    size = width // heads
    w = w_ref[...]
    w_turned = w[:, 2 * width :].T
    lane = lax.broadcasted_iota(jnp.int32, (count, width), 1) // size
    row = lax.broadcasted_iota(jnp.int32, (width, count), 0) // size
    valid = lax.broadcasted_iota(jnp.int32, (count, count), 0) < length_ref[0]
    extra = (v_ref.shape[1] - width, heads * count)
    extra_head = lax.broadcasted_iota(jnp.int32, extra, 1) // count
    ones = jnp.where(lax.broadcasted_iota(jnp.int32, extra, 0) == extra_head, 1.0, 0.0).astype(BF16)
    for j in range(columns):
        normed = normed_ref[j]
        qk = dot(normed, w[:, : 2 * width], 1, 0)
        q = qk[:, :width].astype(BF16)
        vg = dot(w_turned, normed, 1, 1)
        gate_ref[j] = sigmoid(vg[width:])
        v_ref[j, width:, :] = ones
        for h in range(heads):
            own = slice(h * count, (h + 1) * count)
            k = jnp.where(lane == h, qk[:, width:], 0.0).astype(BF16)
            score = dot(k, q, 1, 1) * (size ** (-0.5) * LOG2E)
            score_ref[j, own, :] = jnp.where(valid, score, 0.0)
            v_ref[j, :width, own] = jnp.where(row == h, vg[:width], 0.0).astype(BF16)


def attention_kernel(
    heads, length_ref, bias_ref, score_ref, v_ref, gate_ref, mid_ref, w_ref, out_ref, wide_ref, expo_ref, attended_ref
):
    columns, width, count = gate_ref.shape
    size = width // heads
    blocks = bias_ref.shape[0]
    invalid = lax.broadcasted_iota(jnp.int32, (count, count), 0) >= length_ref[0]
    arrived = bias_ref[...].astype(F32).reshape(blocks, heads, columns, count)
    for h in range(heads):
        own = slice(h * count, (h + 1) * count)
        bias = arrived[:, h].reshape(count, count).T * LOG2E
        bias = jnp.where(invalid, -1000000000.0 * LOG2E, bias)
        tops = []
        for j in range(columns):
            score = score_ref[j, own, :] + bias
            tops.append(jnp.max(score.reshape(-1, 8, count), axis=0))
        tops = [jnp.max(top, axis=0, keepdims=True) for top in tops]
        for j in range(columns):
            expo_ref[j, own, :] = jnp.exp2(score_ref[j, own, :] + bias - tops[j]).astype(BF16)
    for j in range(columns):
        output = dot(v_ref[j], expo_ref[j], 1, 0)
        scale = 1.0 / output[width : width + heads]
        for h in range(heads):
            own = slice(h * size, (h + 1) * size)
            attended = gate_ref[j, own, :] * (output[own] * scale[h : h + 1])
            attended_ref[j, own, :] = attended.astype(BF16)
    w = w_ref[...]
    for j in range(columns):
        result = dot(attended_ref[j], w, 0, 0) + mid_ref[j].astype(F32)
        wide_ref[pl.ds(j, count, stride=columns), :] = result
    out_ref[...] = wide_ref[...].reshape(count, columns, w.shape[1]).astype(BF16)


def call(kernel, outs, operands, specs=None, scratch=(), flops=0):
    size = sum(a.size * a.dtype.itemsize for a in list(operands) + list(outs))
    return pl.pallas_call(
        kernel,
        out_shape=[jax.ShapeDtypeStruct(o.shape, o.dtype) for o in outs],
        in_specs=[VMEM] * len(operands) if specs is None else specs,
        out_specs=[VMEM] * len(outs),
        scratch_shapes=list(scratch),
        cost_estimate=pl.CostEstimate(flops=flops, bytes_accessed=size, transcendentals=0),
        compiler_params=pltpu.CompilerParams(vmem_limit_bytes=24 * 2**20),
    )(*operands)


def shape(dims, dtype):
    return jax.ShapeDtypeStruct(dims, dtype)


def exchange(x):
    return lax.all_to_all(x, "dap", split_axis=0, concat_axis=0, tiled=True)


def kernel_body(pair, w_proj, w_gate_out, w_out, w_qkvg, w_bias, w_att_out, length):
    rows, count, channels = pair.shape
    hidden = w_out.shape[0]
    blocks = count // rows
    heads, width = w_bias.shape[1], w_att_out.shape[0]
    square = (rows, count, channels)
    wide = pltpu.VMEM((rows * count, channels), F32)

    (sent,) = call(
        project_kernel,
        [shape((blocks, 24 * rows, count), BF16)],
        (length, pair, w_proj),
        [SMEM, HBM, HBM],
        [
            pltpu.VMEM(pair.shape, BF16),
            pltpu.VMEM(w_proj.shape, BF16),
            pltpu.SemaphoreType.DMA((1 + rows // 2,)),
        ],
        flops=2 * pair.size * 4 * hidden,
    )
    came = exchange(sent)
    (product,) = call(
        product_kernel,
        [shape((blocks, 8 * rows, count), BF16)],
        (came,),
        scratch=[pltpu.VMEM((blocks * 16 * rows, count), F32)],
        flops=2 * 8 * count**3,
    )
    arrived = exchange(product)
    gate, columns = call(
        gate_kernel,
        [shape(square, F32), shape(square, BF16)],
        (came, w_gate_out),
        scratch=[wide],
        flops=2 * pair.size * channels,
    )
    w_rows = jnp.repeat(w_bias.T, rows, axis=0).astype(F32)
    bias, normed, mid = call(
        middle_kernel,
        [shape((blocks, heads * rows, count), BF16), shape(square, BF16), shape(square, BF16)],
        (arrived, gate, columns, w_out, w_rows),
        scratch=[wide],
        flops=2 * pair.size * channels,
    )
    bias = exchange(bias)
    score, v, gate = call(
        functools.partial(heads_kernel, heads),
        [
            shape((rows, heads * count, count), F32),
            shape((rows, width + 16, heads * count), BF16),
            shape((rows, width, count), F32),
        ],
        (length, normed, w_qkvg),
        [SMEM, VMEM, VMEM],
        flops=2 * pair.size * 8 * width,
    )
    (out,) = call(
        functools.partial(attention_kernel, heads),
        [shape((count, rows, channels), BF16)],
        (length, bias, score, v, gate, mid, w_att_out),
        [SMEM] + [VMEM] * 6,
        [wide, pltpu.VMEM((rows, heads * count, count), BF16), pltpu.VMEM((rows, width, count), BF16)],
        flops=2 * pair.size * count * 8,
    )
    return out


def matmul(spec, a, b):
    return jnp.einsum(spec, a, b, preferred_element_type=jnp.float32)


def whole_body(pair, w_proj, w_gate_out, w_out, w_qkvg, w_bias, w_att_out, length):
    row_count, full_count, channels = pair.shape
    hidden = w_out.shape[0]
    device_count = full_count // row_count
    share = hidden // device_count
    my_index = lax.axis_index("dap")
    positions = jnp.arange(full_count, dtype=jnp.int32)
    valid_keys = (positions < length[0]).astype(jnp.float32)
    row_valid = lax.dynamic_slice_in_dim(valid_keys, my_index * row_count, row_count)

    normed = layer_norm(pair.astype(jnp.float32), 2).astype(jnp.bfloat16)
    projected = matmul("rnc,ce->ern", normed, w_proj)
    pair_mask = row_valid[:, None] * valid_keys[None, :]
    left = jax.nn.sigmoid(projected[hidden : 2 * hidden]) * projected[:hidden] * pair_mask
    right = jax.nn.sigmoid(projected[3 * hidden :]) * projected[2 * hidden : 3 * hidden] * pair_mask
    blocks = (device_count, share * row_count, full_count)
    left = left.astype(jnp.bfloat16).reshape(blocks)
    right = right.astype(jnp.bfloat16).reshape(blocks)
    columns = jnp.transpose(
        pair.reshape(row_count, device_count, row_count, channels), (1, 0, 2, 3)
    )
    cut = share * row_count * full_count
    sent = jnp.concatenate(
        [
            left.reshape(device_count, cut),
            right.reshape(device_count, cut),
            columns.reshape(device_count, row_count * row_count * channels),
        ],
        axis=1,
    )
    came = exchange(sent.reshape(device_count, -1, channels)).reshape(device_count, -1)
    rows = (device_count, share, row_count, full_count)
    left = jnp.transpose(came[:, :cut].reshape(rows), (1, 0, 2, 3))
    right = jnp.transpose(came[:, cut : 2 * cut].reshape(rows), (1, 0, 2, 3))
    columns = came[:, 2 * cut :].reshape(full_count, row_count, channels)

    square = (share, full_count, full_count)
    product = matmul("cjk,cik->cji", right.reshape(square), left.reshape(square))
    product = product.astype(jnp.bfloat16).reshape(share, device_count, row_count, full_count)
    product = exchange(jnp.transpose(product, (1, 0, 2, 3)))
    product = product.reshape(hidden, row_count, full_count)
    product_norm = layer_norm(product.astype(jnp.float32), 0).astype(jnp.bfloat16)
    update = matmul("cji,cd->ijd", product_norm, w_out)
    normed = layer_norm(columns.astype(jnp.float32), 2).astype(jnp.bfloat16)
    gate_out = jax.nn.sigmoid(matmul("ijc,cd->ijd", normed, w_gate_out))
    columns = (columns.astype(jnp.float32) + gate_out * update).astype(jnp.bfloat16)

    normed_mid = layer_norm(columns.astype(jnp.float32), 2).astype(jnp.bfloat16)
    heads = w_bias.shape[1]
    width = w_att_out.shape[0]
    head_size = width // heads
    bias = matmul("kic,ch->hik", normed_mid, w_bias).astype(jnp.bfloat16)
    bias = exchange(jnp.broadcast_to(bias[None], (device_count,) + bias.shape))
    bias = jnp.transpose(bias, (1, 0, 2, 3)).reshape(heads, full_count, full_count)

    mixed = matmul("ijc,ce->ije", normed_mid, w_qkvg)
    per_head = (full_count, row_count, heads, head_size)
    queries = mixed[..., :width].astype(jnp.bfloat16).reshape(per_head)
    keys = mixed[..., width : 2 * width].astype(jnp.bfloat16).reshape(per_head)
    values = mixed[..., 2 * width : 3 * width].astype(jnp.bfloat16).reshape(per_head)
    gate = jax.nn.sigmoid(mixed[..., 3 * width :])
    score = matmul("ijhd,kjhd->jhik", queries, keys) * head_size ** (-0.5)
    score = score + bias.astype(jnp.float32)[None]
    score = jnp.where(valid_keys > 0, score, -1000000000.0)
    top = jnp.max(score, axis=3, keepdims=True)
    expo = jnp.exp(score - top)
    weights = (expo / jnp.sum(expo, axis=3, keepdims=True)).astype(jnp.bfloat16)
    output = matmul("jhik,kjhd->ijhd", weights, values)
    attended = (gate * output.reshape(full_count, row_count, width)).astype(jnp.bfloat16)
    result = columns.astype(jnp.float32) + matmul("ije,ec->ijc", attended, w_att_out)
    return result.astype(jnp.bfloat16)


def body(pair, w_proj, w_gate_out, w_out, w_qkvg, w_bias, w_att_out, length):
    rows, count, channels = pair.shape
    share = w_out.shape[0] * rows // count
    fits = share == rows == 8 and count == channels == w_att_out.shape[0] == 128
    chosen = kernel_body if fits else whole_body
    return chosen(pair, w_proj, w_gate_out, w_out, w_qkvg, w_bias, w_att_out, length)


def solution(mesh):
    placed = (P(("rep", "dap"), None, None), P(), P(), P(), P(), P(), P(), P("rep"))
    return jax.shard_map(
        body, mesh=mesh, in_specs=placed, out_specs=P("rep", "dap", None), check_vma=False
    )
```

```python
import functools

import jax
import jax.numpy as jnp
from jax import lax
from jax.experimental import pallas as pl
from jax.experimental.pallas import tpu as pltpu
from jax.sharding import PartitionSpec as P

VMEM = pl.BlockSpec(memory_space=pltpu.VMEM)
SMEM = pl.BlockSpec(memory_space=pltpu.SMEM)
HBM = pl.BlockSpec(memory_space=pltpu.HBM)
BF16, F32 = jnp.bfloat16, jnp.float32
LOG2E = 1.4426950408889634


def dot(a, b, over_a, over_b):
    return lax.dot_general(a, b, (((over_a,), (over_b,)), ((), ())), preferred_element_type=F32)


def sigmoid(x):
    return 0.5 * jnp.tanh(0.5 * x) + 0.5


def layer_norm(x, axis):
    mean = jnp.mean(x, axis=axis, keepdims=True)
    centered = x - mean
    spread = jnp.mean(centered * centered, axis=axis, keepdims=True)
    return centered * lax.rsqrt(spread + 1e-05)


def interleave(a, b, blocks):
    split = (blocks, a.shape[0] // blocks, a.shape[1])
    return jnp.concatenate([a.reshape(split), b.reshape(split)], axis=1).astype(BF16)


def project_kernel(length_ref, pair_hbm, w_hbm, out_ref, pair_ref, w_ref, sems):
    rows, count, channels = pair_ref.shape
    blocks = out_ref.shape[0]
    hidden = w_ref.shape[1] // 4
    copies = [pltpu.make_async_copy(w_hbm, w_ref, sems.at[0])]
    for r in range(0, rows, 2):
        part = pl.ds(r, 2)
        copies.append(pltpu.make_async_copy(pair_hbm.at[part], pair_ref.at[part], sems.at[1 + r // 2]))
    for copy in copies:
        copy.start()
    first_row = lax.axis_index("dap") * rows
    length = length_ref[0]
    key_valid = jnp.where(lax.broadcasted_iota(jnp.int32, (1, count), 1) < length, 1.0, 0.0)
    for copy in copies:
        copy.wait()
    w_turned = w_ref[...].T
    for r in range(rows):
        x = pair_ref[r].astype(F32)
        normed = layer_norm(x, 1).astype(BF16)
        projected = dot(w_turned, normed, 1, 1)
        mask = key_valid * jnp.where(first_row + r < length, 1.0, 0.0)
        left = sigmoid(projected[hidden : 2 * hidden]) * projected[:hidden] * mask
        right = sigmoid(projected[3 * hidden :]) * projected[2 * hidden : 3 * hidden] * mask
        out_ref[:, 16 * r : 16 * r + 16, :] = interleave(left, right, blocks)
        if r % 2 == 1:
            start = 16 * rows + 8 * (r - 1)
            out_ref[:, start : start + 16, :] = interleave(before, x, blocks)
        before = x


def product_kernel(came_ref, out_ref, wide_ref):
    blocks, per_block, count = out_ref.shape[0], 2 * out_ref.shape[1], out_ref.shape[2]
    for p in range(blocks):
        wide_ref[p * per_block : (p + 1) * per_block, :] = came_ref[p, :per_block].astype(F32)

    def product(c):
        left = wide_ref[pl.ds(c, count, stride=16), :].astype(BF16)
        right = wide_ref[pl.ds(8 + c, count, stride=16), :].astype(BF16)
        return dot(right, left, 1, 1)

    for c in range(0, 8, 2):
        out_ref[:, 8 * c : 8 * c + 16, :] = interleave(product(c), product(c + 1), blocks)


def gate_kernel(came_ref, w_ref, gate_ref, columns_ref, wide_ref):
    columns, count = gate_ref.shape[0], gate_ref.shape[1]
    blocks, per_block = came_ref.shape[0], columns * columns
    for p in range(blocks):
        wide_ref[p * per_block : (p + 1) * per_block, :] = came_ref[p, 2 * per_block :].astype(F32)
    w = w_ref[...]
    for j in range(columns):
        x = wide_ref[pl.ds(j, count, stride=columns), :]
        columns_ref[j] = x.astype(BF16)
        gate_ref[j] = sigmoid(dot(layer_norm(x, 1).astype(BF16), w, 1, 0))


def middle_kernel(came_ref, gate_ref, columns_ref, w_out_ref, w_bias_ref, bias_ref, mid_ref, wide_ref, normed_ref):
    columns, count, channels = mid_ref.shape
    blocks, per_block, _ = came_ref.shape
    hidden = blocks * per_block // columns

    def load(p):
        return came_ref[p].astype(F32).reshape(per_block // columns, columns, count)

    mean = jnp.zeros((columns, count), F32)
    for p in range(blocks):
        mean += jnp.sum(load(p), axis=0)
    mean = mean * (1.0 / hidden)
    spread = jnp.zeros((columns, count), F32)
    for p in range(blocks):
        spread += jnp.sum(jnp.square(load(p) - mean), axis=0)
    scale = lax.rsqrt(spread * (1.0 / hidden) + 1e-05)
    for p in range(blocks):
        part = (load(p) - mean) * scale
        wide_ref[p * per_block : (p + 1) * per_block, :] = part.reshape(per_block, count)
    w_out = w_out_ref[...]
    for j in range(columns):
        product = wide_ref[pl.ds(j, hidden, stride=columns), :].astype(BF16)
        update = dot(product, w_out, 0, 0)
        mid_ref[j] = (columns_ref[j].astype(F32) + gate_ref[j] * update).astype(BF16)
    for j in range(columns):
        normed_ref[j] = layer_norm(mid_ref[j].astype(F32), 1).astype(BF16)
    w_bias = w_bias_ref[...]
    own = lax.broadcasted_iota(jnp.int32, w_bias.shape, 0) % columns
    total = jnp.zeros((w_bias.shape[0], count), F32)
    for j in range(columns):
        total += dot(jnp.where(own == j, w_bias, 0.0).astype(BF16), normed_ref[j], 1, 1)
    bias_ref[...] = jnp.broadcast_to(total.astype(BF16)[None], bias_ref.shape)


def heads_kernel(heads, length_ref, mid_ref, w_ref, score_ref, v_ref, gate_ref):
    columns, count, channels = mid_ref.shape
    width = gate_ref.shape[1]
    size = width // heads
    w = w_ref[...]
    w_turned = w[:, 2 * width :].T
    lane = lax.broadcasted_iota(jnp.int32, (count, width), 1) // size
    valid = lax.broadcasted_iota(jnp.int32, (count, count), 0) < length_ref[0]
    ones = jnp.where(lax.broadcasted_iota(jnp.int32, (16, count), 0) == 0, 1.0, 0.0).astype(BF16)
    for j in range(columns):
        normed = layer_norm(mid_ref[j].astype(F32), 1).astype(BF16)
        qk = dot(normed, w[:, : 2 * width], 1, 0)
        q = qk[:, :width].astype(BF16)
        vg = dot(w_turned, normed, 1, 1)
        gate_ref[j] = sigmoid(vg[width:])
        for h in range(heads):
            own = slice(h * count, (h + 1) * count)
            k = jnp.where(lane == h, qk[:, width:], 0.0).astype(BF16)
            score = dot(k, q, 1, 1) * (size ** (-0.5) * LOG2E)
            score_ref[j, own, :] = jnp.where(valid, score, 0.0)
            v_ref[j, h, :size, :] = vg[h * size : (h + 1) * size].astype(BF16)
            v_ref[j, h, size:, :] = ones


def attention_kernel(
    heads, length_ref, bias_ref, score_ref, v_ref, gate_ref, mid_ref, w_ref, out_ref, wide_ref, expo_ref, attended_ref
):
    columns, width, count = gate_ref.shape
    size = width // heads
    blocks = bias_ref.shape[0]
    invalid = lax.broadcasted_iota(jnp.int32, (count, count), 0) >= length_ref[0]
    arrived = bias_ref[...].astype(F32).reshape(blocks, heads, columns, count)
    for h in range(heads):
        own = slice(h * count, (h + 1) * count)
        bias = arrived[:, h].reshape(count, count).T * LOG2E
        bias = jnp.where(invalid, -1000000000.0 * LOG2E, bias)
        tops = []
        for j in range(columns):
            score = score_ref[j, own, :] + bias
            tops.append(jnp.max(score.reshape(-1, 8, count), axis=0))
        tops = [jnp.max(top, axis=0, keepdims=True) for top in tops]
        for j in range(columns):
            expo_ref[j, own, :] = jnp.exp2(score_ref[j, own, :] + bias - tops[j]).astype(BF16)
    for j in range(columns):
        for h in range(heads):
            own = slice(h * size, (h + 1) * size)
            output = dot(v_ref[j, h], expo_ref[j, h * count : (h + 1) * count, :], 1, 0)
            attended = gate_ref[j, own, :] * (output[:size] * (1.0 / output[size : size + 1]))
            attended_ref[j, own, :] = attended.astype(BF16)
    w = w_ref[...]
    for j in range(columns):
        result = dot(attended_ref[j], w, 0, 0) + mid_ref[j].astype(F32)
        wide_ref[pl.ds(j, count, stride=columns), :] = result
    out_ref[...] = wide_ref[...].reshape(count, columns, w.shape[1]).astype(BF16)


def call(kernel, outs, operands, specs=None, scratch=(), flops=0):
    size = sum(a.size * a.dtype.itemsize for a in list(operands) + list(outs))
    return pl.pallas_call(
        kernel,
        out_shape=[jax.ShapeDtypeStruct(o.shape, o.dtype) for o in outs],
        in_specs=[VMEM] * len(operands) if specs is None else specs,
        out_specs=[VMEM] * len(outs),
        scratch_shapes=list(scratch),
        cost_estimate=pl.CostEstimate(flops=flops, bytes_accessed=size, transcendentals=0),
        compiler_params=pltpu.CompilerParams(vmem_limit_bytes=24 * 2**20),
    )(*operands)


def shape(dims, dtype):
    return jax.ShapeDtypeStruct(dims, dtype)


def exchange(x):
    return lax.all_to_all(x, "dap", split_axis=0, concat_axis=0, tiled=True)


def kernel_body(pair, w_proj, w_gate_out, w_out, w_qkvg, w_bias, w_att_out, length):
    rows, count, channels = pair.shape
    hidden = w_out.shape[0]
    blocks = count // rows
    heads, width = w_bias.shape[1], w_att_out.shape[0]
    square = (rows, count, channels)
    wide = pltpu.VMEM((rows * count, channels), F32)

    (sent,) = call(
        project_kernel,
        [shape((blocks, 24 * rows, count), BF16)],
        (
            length,
            pltpu.with_memory_space_constraint(pair, pltpu.HBM),
            pltpu.with_memory_space_constraint(w_proj, pltpu.HBM),
        ),
        [SMEM, HBM, HBM],
        [
            pltpu.VMEM(pair.shape, BF16),
            pltpu.VMEM(w_proj.shape, BF16),
            pltpu.SemaphoreType.DMA((1 + rows // 2,)),
        ],
        flops=2 * pair.size * 4 * hidden,
    )
    came = exchange(sent)
    (product,) = call(
        product_kernel,
        [shape((blocks, 8 * rows, count), BF16)],
        (came,),
        scratch=[pltpu.VMEM((blocks * 16 * rows, count), F32)],
        flops=2 * 8 * count**3,
    )
    arrived = exchange(product)
    gate, columns = call(
        gate_kernel,
        [shape(square, F32), shape(square, BF16)],
        (came, w_gate_out),
        scratch=[wide],
        flops=2 * pair.size * channels,
    )
    w_rows = jnp.repeat(w_bias.T, rows, axis=0).astype(F32)
    bias, mid = call(
        middle_kernel,
        [shape((blocks, heads * rows, count), BF16), shape(square, BF16)],
        (arrived, gate, columns, w_out, w_rows),
        scratch=[wide, pltpu.VMEM(square, BF16)],
        flops=2 * pair.size * channels,
    )
    bias = exchange(bias)
    score, v, gate = call(
        functools.partial(heads_kernel, heads),
        [
            shape((rows, heads * count, count), F32),
            shape((rows, heads, width // heads + 16, count), BF16),
            shape((rows, width, count), F32),
        ],
        (length, mid, w_qkvg),
        [SMEM, VMEM, VMEM],
        flops=2 * pair.size * 8 * width,
    )
    (out,) = call(
        functools.partial(attention_kernel, heads),
        [shape((count, rows, channels), BF16)],
        (length, bias, score, v, gate, mid, w_att_out),
        [SMEM] + [VMEM] * 6,
        [wide, pltpu.VMEM((rows, heads * count, count), BF16), pltpu.VMEM((rows, width, count), BF16)],
        flops=2 * pair.size * count * 8,
    )
    return out


def matmul(spec, a, b):
    return jnp.einsum(spec, a, b, preferred_element_type=jnp.float32)


def whole_body(pair, w_proj, w_gate_out, w_out, w_qkvg, w_bias, w_att_out, length):
    row_count, full_count, channels = pair.shape
    hidden = w_out.shape[0]
    device_count = full_count // row_count
    share = hidden // device_count
    my_index = lax.axis_index("dap")
    positions = jnp.arange(full_count, dtype=jnp.int32)
    valid_keys = (positions < length[0]).astype(jnp.float32)
    row_valid = lax.dynamic_slice_in_dim(valid_keys, my_index * row_count, row_count)

    normed = layer_norm(pair.astype(jnp.float32), 2).astype(jnp.bfloat16)
    projected = matmul("rnc,ce->ern", normed, w_proj)
    pair_mask = row_valid[:, None] * valid_keys[None, :]
    left = jax.nn.sigmoid(projected[hidden : 2 * hidden]) * projected[:hidden] * pair_mask
    right = jax.nn.sigmoid(projected[3 * hidden :]) * projected[2 * hidden : 3 * hidden] * pair_mask
    blocks = (device_count, share * row_count, full_count)
    left = left.astype(jnp.bfloat16).reshape(blocks)
    right = right.astype(jnp.bfloat16).reshape(blocks)
    columns = jnp.transpose(
        pair.reshape(row_count, device_count, row_count, channels), (1, 0, 2, 3)
    )
    cut = share * row_count * full_count
    sent = jnp.concatenate(
        [
            left.reshape(device_count, cut),
            right.reshape(device_count, cut),
            columns.reshape(device_count, row_count * row_count * channels),
        ],
        axis=1,
    )
    came = exchange(sent.reshape(device_count, -1, channels)).reshape(device_count, -1)
    rows = (device_count, share, row_count, full_count)
    left = jnp.transpose(came[:, :cut].reshape(rows), (1, 0, 2, 3))
    right = jnp.transpose(came[:, cut : 2 * cut].reshape(rows), (1, 0, 2, 3))
    columns = came[:, 2 * cut :].reshape(full_count, row_count, channels)

    square = (share, full_count, full_count)
    product = matmul("cjk,cik->cji", right.reshape(square), left.reshape(square))
    product = product.astype(jnp.bfloat16).reshape(share, device_count, row_count, full_count)
    product = exchange(jnp.transpose(product, (1, 0, 2, 3)))
    product = product.reshape(hidden, row_count, full_count)
    product_norm = layer_norm(product.astype(jnp.float32), 0).astype(jnp.bfloat16)
    update = matmul("cji,cd->ijd", product_norm, w_out)
    normed = layer_norm(columns.astype(jnp.float32), 2).astype(jnp.bfloat16)
    gate_out = jax.nn.sigmoid(matmul("ijc,cd->ijd", normed, w_gate_out))
    columns = (columns.astype(jnp.float32) + gate_out * update).astype(jnp.bfloat16)

    normed_mid = layer_norm(columns.astype(jnp.float32), 2).astype(jnp.bfloat16)
    heads = w_bias.shape[1]
    width = w_att_out.shape[0]
    head_size = width // heads
    bias = matmul("kic,ch->hik", normed_mid, w_bias).astype(jnp.bfloat16)
    bias = exchange(jnp.broadcast_to(bias[None], (device_count,) + bias.shape))
    bias = jnp.transpose(bias, (1, 0, 2, 3)).reshape(heads, full_count, full_count)

    mixed = matmul("ijc,ce->ije", normed_mid, w_qkvg)
    per_head = (full_count, row_count, heads, head_size)
    queries = mixed[..., :width].astype(jnp.bfloat16).reshape(per_head)
    keys = mixed[..., width : 2 * width].astype(jnp.bfloat16).reshape(per_head)
    values = mixed[..., 2 * width : 3 * width].astype(jnp.bfloat16).reshape(per_head)
    gate = jax.nn.sigmoid(mixed[..., 3 * width :])
    score = matmul("ijhd,kjhd->jhik", queries, keys) * head_size ** (-0.5)
    score = score + bias.astype(jnp.float32)[None]
    score = jnp.where(valid_keys > 0, score, -1000000000.0)
    top = jnp.max(score, axis=3, keepdims=True)
    expo = jnp.exp(score - top)
    weights = (expo / jnp.sum(expo, axis=3, keepdims=True)).astype(jnp.bfloat16)
    output = matmul("jhik,kjhd->ijhd", weights, values)
    attended = (gate * output.reshape(full_count, row_count, width)).astype(jnp.bfloat16)
    result = columns.astype(jnp.float32) + matmul("ije,ec->ijc", attended, w_att_out)
    return result.astype(jnp.bfloat16)


def body(pair, w_proj, w_gate_out, w_out, w_qkvg, w_bias, w_att_out, length):
    rows, count, channels = pair.shape
    share = w_out.shape[0] * rows // count
    fits = share == rows == 8 and count == channels == w_att_out.shape[0] == 128
    chosen = kernel_body if fits else whole_body
    return chosen(pair, w_proj, w_gate_out, w_out, w_qkvg, w_bias, w_att_out, length)


def solution(mesh):
    placed = (P(("rep", "dap"), None, None), P(), P(), P(), P(), P(), P(), P("rep"))
    return jax.shard_map(
        body, mesh=mesh, in_specs=placed, out_specs=P("rep", "dap", None), check_vma=False
    )
```

```python
import functools

import jax
import jax.numpy as jnp
from jax import lax
from jax.experimental import pallas as pl
from jax.experimental.pallas import tpu as pltpu
from jax.sharding import PartitionSpec as P

VMEM = pl.BlockSpec(memory_space=pltpu.VMEM)
SMEM = pl.BlockSpec(memory_space=pltpu.SMEM)
HBM = pl.BlockSpec(memory_space=pltpu.HBM)
BF16, F32 = jnp.bfloat16, jnp.float32
LOG2E = 1.4426950408889634


def dot(a, b, over_a, over_b):
    return lax.dot_general(a, b, (((over_a,), (over_b,)), ((), ())), preferred_element_type=F32)


def sigmoid(x):
    return 0.5 * jnp.tanh(0.5 * x) + 0.5


def layer_norm(x, axis):
    mean = jnp.mean(x, axis=axis, keepdims=True)
    centered = x - mean
    spread = jnp.mean(centered * centered, axis=axis, keepdims=True)
    return centered * lax.rsqrt(spread + 1e-05)


def interleave(a, b, blocks):
    split = (blocks, a.shape[0] // blocks, a.shape[1])
    return jnp.concatenate([a.reshape(split), b.reshape(split)], axis=1).astype(BF16)


def project_kernel(
    length_ref,
    pair_hbm,
    w_hbm,
    w_gate_hbm,
    w_bias_hbm,
    out_ref,
    gate_ref,
    w_rows_ref,
    pair_ref,
    w_ref,
    w_gate_ref,
    w_bias_ref,
    normed_ref,
    sems,
):
    rows, count, channels = pair_ref.shape
    blocks = out_ref.shape[0]
    hidden = w_ref.shape[1] // 4
    copies = [
        pltpu.make_async_copy(pair_hbm, pair_ref, sems.at[0]),
        pltpu.make_async_copy(w_hbm, w_ref, sems.at[1]),
        pltpu.make_async_copy(w_gate_hbm, w_gate_ref, sems.at[2]),
        pltpu.make_async_copy(w_bias_hbm, w_bias_ref, sems.at[3]),
    ]
    for copy in copies:
        copy.start()
    first_row = lax.axis_index("dap") * rows
    length = length_ref[0]
    key_valid = jnp.where(lax.broadcasted_iota(jnp.int32, (1, count), 1) < length, 1.0, 0.0)
    for copy in copies:
        copy.wait()
    for r in range(rows):
        normed_ref[r] = layer_norm(pair_ref[r].astype(F32), 1).astype(BF16)
    w_turned = w_ref[...].T
    for r in range(rows):
        projected = dot(w_turned, normed_ref[r], 1, 1)
        mask = key_valid * jnp.where(first_row + r < length, 1.0, 0.0)
        left = sigmoid(projected[hidden : 2 * hidden]) * projected[:hidden] * mask
        right = sigmoid(projected[3 * hidden :]) * projected[2 * hidden : 3 * hidden] * mask
        out_ref[:, 16 * r : 16 * r + 16, :] = interleave(left, right, blocks)
    w_gate = w_gate_ref[...]
    for r in range(rows):
        gate_ref[r] = sigmoid(dot(normed_ref[r], w_gate, 1, 0))
    w_bias = w_bias_ref[...].astype(F32)
    for h in range(w_bias.shape[0]):
        w_rows_ref[h * rows : (h + 1) * rows, :] = jnp.broadcast_to(w_bias[h : h + 1], (rows, channels))


def product_kernel(came_ref, out_ref, wide_ref):
    blocks, per_block, count = came_ref.shape
    for p in range(blocks):
        wide_ref[p * per_block : (p + 1) * per_block, :] = came_ref[p].astype(F32)

    def product(c):
        left = wide_ref[pl.ds(c, count, stride=16), :].astype(BF16)
        right = wide_ref[pl.ds(8 + c, count, stride=16), :].astype(BF16)
        return dot(left, right, 1, 1)

    for c in range(0, 8, 2):
        out_ref[:, 8 * c : 8 * c + 16, :] = interleave(product(c), product(c + 1), blocks)


def middle_kernel(came_ref, gate_ref, pair_ref, w_out_ref, w_rows_ref, out_ref, wide_ref, mid_ref, normed_ref):
    rows, count, channels = pair_ref.shape
    blocks, per_block, _ = came_ref.shape
    hidden = blocks * per_block // rows

    def load(p):
        return came_ref[p].astype(F32).reshape(per_block // rows, rows, count)

    mean = jnp.zeros((rows, count), F32)
    for p in range(blocks):
        mean += jnp.sum(load(p), axis=0)
    mean = mean * (1.0 / hidden)
    spread = jnp.zeros((rows, count), F32)
    for p in range(blocks):
        spread += jnp.sum(jnp.square(load(p) - mean), axis=0)
    scale = lax.rsqrt(spread * (1.0 / hidden) + 1e-05)
    for p in range(blocks):
        part = (load(p) - mean) * scale
        wide_ref[p * per_block : (p + 1) * per_block, :] = part.reshape(per_block, count)
    w_out = w_out_ref[...]
    for r in range(rows):
        product = wide_ref[pl.ds(r, hidden, stride=rows), :].astype(BF16)
        update = dot(product, w_out, 0, 0)
        mid = (pair_ref[r].astype(F32) + gate_ref[r] * update).astype(BF16)
        mid_ref[r] = mid.astype(F32)
    for r in range(0, rows, 2):
        out_ref[:, 8 * r : 8 * r + 16, :] = interleave(mid_ref[r], mid_ref[r + 1], blocks)
    for r in range(rows):
        normed_ref[r] = layer_norm(mid_ref[r], 1).astype(BF16)
    w_bias = w_rows_ref[...]
    own = lax.broadcasted_iota(jnp.int32, w_bias.shape, 0) % rows
    bias = jnp.zeros((w_bias.shape[0], count), F32)
    for r in range(rows):
        bias += dot(jnp.where(own == r, w_bias, 0.0).astype(BF16), normed_ref[r], 1, 1)
    out_ref[:, 8 * rows :, :] = jnp.broadcast_to(bias.astype(BF16)[None], (blocks,) + bias.shape)


def attention_kernel(
    heads,
    length_ref,
    came_ref,
    w_ref,
    w_out_ref,
    out_ref,
    wide_ref,
    added_ref,
    normed_ref,
    q_ref,
    k_ref,
    v_ref,
    gate_ref,
    score_ref,
    expo_ref,
    attended_ref,
):
    columns, width, count = gate_ref.shape
    size = width // heads
    blocks, block = came_ref.shape[0], columns * columns
    for p in range(blocks):
        wide_ref[p * block : (p + 1) * block, :] = came_ref[p, :block].astype(F32)
    for j in range(columns):
        normed_ref[j] = layer_norm(wide_ref[pl.ds(j, count, stride=columns), :], 1).astype(BF16)
    w = w_ref[...]
    for j in range(columns):
        qk = dot(normed_ref[j], w[:, : 2 * width], 1, 0)
        q_ref[j] = qk[:, :width].astype(BF16)
        k_ref[j] = qk[:, width:].astype(BF16)
    w_turned = w[:, 2 * width :].T
    ones = jnp.where(lax.broadcasted_iota(jnp.int32, (16, count), 0) == 0, 1.0, 0.0).astype(BF16)
    for j in range(columns):
        vg = dot(w_turned, normed_ref[j], 1, 1)
        gate_ref[j] = sigmoid(vg[width:])
        for h in range(heads):
            v_ref[j, h, :size, :] = vg[h * size : (h + 1) * size].astype(BF16)
            v_ref[j, h, size:, :] = ones
    lane = lax.broadcasted_iota(jnp.int32, (count, width), 1) // size
    valid = lax.broadcasted_iota(jnp.int32, (count, count), 0) < length_ref[0]
    for h in range(heads):
        own = slice(h * count, (h + 1) * count)
        start = block + h * columns
        bias = came_ref[:, start : start + columns, :].astype(F32).reshape(count, count) * LOG2E
        own_lanes = jnp.where(lane == h, 1.0, 0.0).astype(BF16)
        for j in range(columns):
            scaled = dot(k_ref[j] * own_lanes, q_ref[j], 1, 1) * (size ** (-0.5) * LOG2E) + bias
            score_ref[j, own, :] = jnp.where(valid, scaled, -1000000000.0 * LOG2E)
    for h in range(heads):
        own = slice(h * count, (h + 1) * count)
        tops = [jnp.max(score_ref[j, own, :].reshape(-1, 8, count), axis=0) for j in range(columns)]
        tops = [jnp.max(top, axis=0, keepdims=True) for top in tops]
        for j in range(columns):
            expo_ref[j, own, :] = jnp.exp2(score_ref[j, own, :] - tops[j]).astype(BF16)
    for j in range(columns):
        for h in range(heads):
            own = slice(h * size, (h + 1) * size)
            output = dot(v_ref[j, h], expo_ref[j, h * count : (h + 1) * count, :], 1, 0)
            attended = gate_ref[j, own, :] * (output[:size] * (1.0 / output[size : size + 1]))
            attended_ref[j, own, :] = attended.astype(BF16)
    w_out = w_out_ref[...]
    for j in range(columns):
        added_ref[pl.ds(j, count, stride=columns), :] = dot(attended_ref[j], w_out, 0, 0)
    out_ref[...] = (wide_ref[...] + added_ref[...]).reshape(count, columns, w_out.shape[1]).astype(BF16)


def call(kernel, outs, operands, specs=None, scratch=()):
    size = sum(a.size * a.dtype.itemsize for a in list(operands) + list(outs))
    return pl.pallas_call(
        kernel,
        out_shape=[jax.ShapeDtypeStruct(o.shape, o.dtype) for o in outs],
        in_specs=[VMEM] * len(operands) if specs is None else specs,
        out_specs=[VMEM] * len(outs),
        scratch_shapes=list(scratch),
        cost_estimate=pl.CostEstimate(flops=0, bytes_accessed=size, transcendentals=0),
        compiler_params=pltpu.CompilerParams(vmem_limit_bytes=24 * 2**20),
    )(*operands)


def shape(dims, dtype):
    return jax.ShapeDtypeStruct(dims, dtype)


def exchange(x):
    return lax.all_to_all(x, "dap", split_axis=0, concat_axis=0, tiled=True)


def kernel_body(pair, w_proj, w_gate_out, w_out, w_qkvg, w_bias, w_att_out, length):
    rows, count, channels = pair.shape
    hidden = w_out.shape[0]
    blocks = count // rows
    heads, width = w_bias.shape[1], w_att_out.shape[0]
    square = (rows, count, channels)
    wide = pltpu.VMEM((rows * count, channels), F32)

    sent, gate, w_rows = call(
        project_kernel,
        [shape((blocks, 16 * rows, count), BF16), shape(square, F32), shape((heads * rows, channels), F32)],
        [length] + [pltpu.with_memory_space_constraint(x, pltpu.HBM) for x in (pair, w_proj, w_gate_out, w_bias.T)],
        [SMEM] + [HBM] * 4,
        [
            pltpu.VMEM(pair.shape, BF16),
            pltpu.VMEM(w_proj.shape, BF16),
            pltpu.VMEM(w_gate_out.shape, BF16),
            pltpu.VMEM((heads, channels), BF16),
            pltpu.VMEM(square, BF16),
            pltpu.SemaphoreType.DMA((4,)),
        ],
    )
    came = exchange(sent)
    (product,) = call(
        product_kernel,
        [shape((blocks, 8 * rows, count), BF16)],
        (came,),
        scratch=[pltpu.VMEM((blocks * 16 * rows, count), F32)],
    )
    came = exchange(product)
    (sent,) = call(
        middle_kernel,
        [shape((blocks, (8 + heads) * rows, count), BF16)],
        (came, gate, pair, w_out, w_rows),
        scratch=[wide, pltpu.VMEM(square, F32), pltpu.VMEM(square, BF16)],
    )
    came = exchange(sent)
    (out,) = call(
        functools.partial(attention_kernel, heads),
        [shape((count, rows, channels), BF16)],
        (length, came, w_qkvg, w_att_out),
        [SMEM] + [VMEM] * 3,
        [
            wide,
            wide,
            pltpu.VMEM(square, BF16),
            pltpu.VMEM((rows, count, width), BF16),
            pltpu.VMEM((rows, count, width), BF16),
            pltpu.VMEM((rows, heads, width // heads + 16, count), BF16),
            pltpu.VMEM((rows, width, count), F32),
            pltpu.VMEM((rows, heads * count, count), F32),
            pltpu.VMEM((rows, heads * count, count), BF16),
            pltpu.VMEM((rows, width, count), BF16),
        ],
    )
    return out


def matmul(spec, a, b):
    return jnp.einsum(spec, a, b, preferred_element_type=jnp.float32)


def whole_body(pair, w_proj, w_gate_out, w_out, w_qkvg, w_bias, w_att_out, length):
    row_count, full_count, channels = pair.shape
    hidden = w_out.shape[0]
    device_count = full_count // row_count
    share = hidden // device_count
    my_index = lax.axis_index("dap")
    positions = jnp.arange(full_count, dtype=jnp.int32)
    valid_keys = (positions < length[0]).astype(jnp.float32)
    row_valid = lax.dynamic_slice_in_dim(valid_keys, my_index * row_count, row_count)

    normed = layer_norm(pair.astype(jnp.float32), 2).astype(jnp.bfloat16)
    projected = matmul("rnc,ce->ern", normed, w_proj)
    pair_mask = row_valid[:, None] * valid_keys[None, :]
    left = jax.nn.sigmoid(projected[hidden : 2 * hidden]) * projected[:hidden] * pair_mask
    right = jax.nn.sigmoid(projected[3 * hidden :]) * projected[2 * hidden : 3 * hidden] * pair_mask
    blocks = (device_count, share * row_count, full_count)
    left = left.astype(jnp.bfloat16).reshape(blocks)
    right = right.astype(jnp.bfloat16).reshape(blocks)
    columns = jnp.transpose(
        pair.reshape(row_count, device_count, row_count, channels), (1, 0, 2, 3)
    )
    cut = share * row_count * full_count
    sent = jnp.concatenate(
        [
            left.reshape(device_count, cut),
            right.reshape(device_count, cut),
            columns.reshape(device_count, row_count * row_count * channels),
        ],
        axis=1,
    )
    came = exchange(sent.reshape(device_count, -1, channels)).reshape(device_count, -1)
    rows = (device_count, share, row_count, full_count)
    left = jnp.transpose(came[:, :cut].reshape(rows), (1, 0, 2, 3))
    right = jnp.transpose(came[:, cut : 2 * cut].reshape(rows), (1, 0, 2, 3))
    columns = came[:, 2 * cut :].reshape(full_count, row_count, channels)

    square = (share, full_count, full_count)
    product = matmul("cjk,cik->cji", right.reshape(square), left.reshape(square))
    product = product.astype(jnp.bfloat16).reshape(share, device_count, row_count, full_count)
    product = exchange(jnp.transpose(product, (1, 0, 2, 3)))
    product = product.reshape(hidden, row_count, full_count)
    product_norm = layer_norm(product.astype(jnp.float32), 0).astype(jnp.bfloat16)
    update = matmul("cji,cd->ijd", product_norm, w_out)
    normed = layer_norm(columns.astype(jnp.float32), 2).astype(jnp.bfloat16)
    gate_out = jax.nn.sigmoid(matmul("ijc,cd->ijd", normed, w_gate_out))
    columns = (columns.astype(jnp.float32) + gate_out * update).astype(jnp.bfloat16)

    normed_mid = layer_norm(columns.astype(jnp.float32), 2).astype(jnp.bfloat16)
    heads = w_bias.shape[1]
    width = w_att_out.shape[0]
    head_size = width // heads
    bias = matmul("kic,ch->hik", normed_mid, w_bias).astype(jnp.bfloat16)
    bias = exchange(jnp.broadcast_to(bias[None], (device_count,) + bias.shape))
    bias = jnp.transpose(bias, (1, 0, 2, 3)).reshape(heads, full_count, full_count)

    mixed = matmul("ijc,ce->ije", normed_mid, w_qkvg)
    per_head = (full_count, row_count, heads, head_size)
    queries = mixed[..., :width].astype(jnp.bfloat16).reshape(per_head)
    keys = mixed[..., width : 2 * width].astype(jnp.bfloat16).reshape(per_head)
    values = mixed[..., 2 * width : 3 * width].astype(jnp.bfloat16).reshape(per_head)
    gate = jax.nn.sigmoid(mixed[..., 3 * width :])
    score = matmul("ijhd,kjhd->jhik", queries, keys) * head_size ** (-0.5)
    score = score + bias.astype(jnp.float32)[None]
    score = jnp.where(valid_keys > 0, score, -1000000000.0)
    top = jnp.max(score, axis=3, keepdims=True)
    expo = jnp.exp(score - top)
    weights = (expo / jnp.sum(expo, axis=3, keepdims=True)).astype(jnp.bfloat16)
    output = matmul("jhik,kjhd->ijhd", weights, values)
    attended = (gate * output.reshape(full_count, row_count, width)).astype(jnp.bfloat16)
    result = columns.astype(jnp.float32) + matmul("ije,ec->ijc", attended, w_att_out)
    return result.astype(jnp.bfloat16)


def body(pair, w_proj, w_gate_out, w_out, w_qkvg, w_bias, w_att_out, length):
    rows, count, channels = pair.shape
    share = w_out.shape[0] * rows // count
    fits = share == rows == 8 and count == channels == w_att_out.shape[0] == 128
    chosen = kernel_body if fits else whole_body
    return chosen(pair, w_proj, w_gate_out, w_out, w_qkvg, w_bias, w_att_out, length)


def solution(mesh):
    placed = (P(("rep", "dap"), None, None), P(), P(), P(), P(), P(), P(), P("rep"))
    return jax.shard_map(
        body, mesh=mesh, in_specs=placed, out_specs=P("rep", "dap", None), check_vma=False
    )
```

```python
import functools

import jax
import jax.numpy as jnp
from jax import lax
from jax.experimental import pallas as pl
from jax.experimental.pallas import tpu as pltpu
from jax.sharding import PartitionSpec as P

VMEM = pl.BlockSpec(memory_space=pltpu.VMEM)
SMEM = pl.BlockSpec(memory_space=pltpu.SMEM)
HBM = pl.BlockSpec(memory_space=pltpu.HBM)
BF16, F32 = jnp.bfloat16, jnp.float32
LOG2E = 1.4426950408889634
ORDER = [4, 0, 12, 8, 14, 10, 6, 2, 5, 1, 13, 9, 15, 11, 7, 3]


def dot(a, b, over_a, over_b):
    return lax.dot_general(a, b, (((over_a,), (over_b,)), ((), ())), preferred_element_type=F32)


def sigmoid(x):
    return 0.5 * jnp.tanh(0.5 * x) + 0.5


def layer_norm(x, axis):
    mean = jnp.mean(x, axis=axis, keepdims=True)
    centered = x - mean
    spread = jnp.mean(centered * centered, axis=axis, keepdims=True)
    return centered * lax.rsqrt(spread + 1e-05)


def by_block(x, order):
    size = x.shape[0] // len(order)
    return jnp.concatenate([x[d * size : (d + 1) * size] for d in order], axis=0)


def interleave(a, b, blocks):
    split = (blocks, a.shape[0] // blocks, a.shape[1])
    return jnp.concatenate([a.reshape(split), b.reshape(split)], axis=1).astype(BF16)


def project_kernel(
    length_ref,
    pair_hbm,
    w_hbm,
    w_gate_hbm,
    w_bias_hbm,
    out_ref,
    gate_ref,
    w_rows_ref,
    pair_ref,
    w_ref,
    w_gate_ref,
    w_bias_ref,
    normed_ref,
    sems,
):
    rows, count, channels = pair_ref.shape
    blocks = out_ref.shape[0]
    hidden = w_ref.shape[1] // 4
    copies = [
        pltpu.make_async_copy(pair_hbm, pair_ref, sems.at[0]),
        pltpu.make_async_copy(w_hbm, w_ref, sems.at[1]),
        pltpu.make_async_copy(w_gate_hbm, w_gate_ref, sems.at[2]),
        pltpu.make_async_copy(w_bias_hbm, w_bias_ref, sems.at[3]),
    ]
    for copy in copies:
        copy.start()
    first_row = lax.axis_index("dap") * rows
    length = length_ref[0]
    key_valid = jnp.where(lax.broadcasted_iota(jnp.int32, (1, count), 1) < length, 1.0, 0.0)
    for copy in copies:
        copy.wait()
    for r in range(rows):
        normed_ref[r] = layer_norm(pair_ref[r].astype(F32), 1).astype(BF16)
    w_turned = w_ref[...].T
    for r in range(rows):
        projected = dot(w_turned, normed_ref[r], 1, 1)
        mask = key_valid * jnp.where(first_row + r < length, 1.0, 0.0)
        left = sigmoid(projected[hidden : 2 * hidden]) * projected[:hidden] * mask
        right = sigmoid(projected[3 * hidden :]) * projected[2 * hidden : 3 * hidden] * mask
        out_ref[:, 16 * r : 16 * r + 16, :] = interleave(left, right, blocks)
    w_gate = w_gate_ref[...]
    for r in range(rows):
        gate_ref[r] = sigmoid(dot(normed_ref[r], w_gate, 1, 0))
    w_bias = w_bias_ref[...].astype(F32)
    for h in range(w_bias.shape[0]):
        w_rows_ref[h * rows : (h + 1) * rows, :] = jnp.broadcast_to(w_bias[h : h + 1], (rows, channels))


def product_kernel(came_ref, out_ref, wide_ref):
    blocks, per_block, count = came_ref.shape
    for p in range(blocks):
        wide_ref[p * per_block : (p + 1) * per_block, :] = came_ref[p].astype(F32)

    def product(c):
        left = wide_ref[pl.ds(c, count, stride=16), :].astype(BF16)
        right = wide_ref[pl.ds(8 + c, count, stride=16), :].astype(BF16)
        return dot(left, right, 1, 1)

    for c in range(0, 8, 2):
        out_ref[:, 8 * c : 8 * c + 16, :] = interleave(product(c), product(c + 1), blocks)


def middle_kernel(order, came_ref, gate_ref, pair_ref, w_out_ref, w_rows_ref, out_ref, wide_ref, mid_ref, normed_ref):
    rows, count, channels = pair_ref.shape
    blocks, per_block, _ = came_ref.shape
    hidden = blocks * per_block // rows

    def load(p):
        return came_ref[p].astype(F32).reshape(per_block // rows, rows, count)

    mean = jnp.zeros((rows, count), F32)
    for p in range(blocks):
        mean += jnp.sum(load(p), axis=0)
    mean = mean * (1.0 / hidden)
    spread = jnp.zeros((rows, count), F32)
    for p in range(blocks):
        spread += jnp.sum(jnp.square(load(p) - mean), axis=0)
    scale = lax.rsqrt(spread * (1.0 / hidden) + 1e-05)
    for p in range(blocks):
        part = (load(p) - mean) * scale
        wide_ref[p * per_block : (p + 1) * per_block, :] = part.reshape(per_block, count)
    w_out = w_out_ref[...]
    for r in range(rows):
        product = wide_ref[pl.ds(r, hidden, stride=rows), :].astype(BF16)
        update = dot(product, w_out, 0, 0)
        pair, gate = by_block(pair_ref[r].astype(F32), order), by_block(gate_ref[r], order)
        mid = (pair + gate * update).astype(BF16)
        mid_ref[r] = mid.astype(F32)
    for r in range(0, rows, 2):
        out_ref[:, 8 * r : 8 * r + 16, :] = interleave(mid_ref[r], mid_ref[r + 1], blocks)
    for r in range(rows):
        normed_ref[r] = layer_norm(mid_ref[r], 1).astype(BF16)
    w_bias = w_rows_ref[...]
    own = lax.broadcasted_iota(jnp.int32, w_bias.shape, 0) % rows
    bias = jnp.zeros((w_bias.shape[0], count), F32)
    for r in range(rows):
        bias += dot(jnp.where(own == r, w_bias, 0.0).astype(BF16), normed_ref[r], 1, 1)
    out_ref[:, 8 * rows :, :] = jnp.broadcast_to(bias.astype(BF16)[None], (blocks,) + bias.shape)


def attention_kernel(
    order,
    heads,
    length_ref,
    came_ref,
    w_ref,
    w_out_ref,
    out_ref,
    wide_ref,
    added_ref,
    normed_ref,
    q_ref,
    k_ref,
    v_ref,
    gate_ref,
    score_ref,
    expo_ref,
    attended_ref,
):
    columns, width, count = gate_ref.shape
    size = width // heads
    blocks, block = came_ref.shape[0], columns * columns
    for p in range(blocks):
        wide_ref[p * block : (p + 1) * block, :] = came_ref[p, :block].astype(F32)
    for j in range(columns):
        normed_ref[j] = layer_norm(wide_ref[pl.ds(j, count, stride=columns), :], 1).astype(BF16)
    w = w_ref[...]
    for j in range(columns):
        qk = dot(normed_ref[j], w[:, : 2 * width], 1, 0)
        q_ref[j] = qk[:, :width].astype(BF16)
        k_ref[j] = qk[:, width:].astype(BF16)
    w_turned = w[:, 2 * width :].T
    ones = jnp.where(lax.broadcasted_iota(jnp.int32, (16, count), 0) == 0, 1.0, 0.0).astype(BF16)
    for j in range(columns):
        vg = dot(w_turned, normed_ref[j], 1, 1)
        gate_ref[j] = sigmoid(vg[width:])
        for h in range(heads):
            v_ref[j, h, :size, :] = vg[h * size : (h + 1) * size].astype(BF16)
            v_ref[j, h, size:, :] = ones
    lane = lax.broadcasted_iota(jnp.int32, (count, width), 1) // size
    token = by_block(lax.broadcasted_iota(jnp.int32, (count, count), 0), order)
    valid = token < length_ref[0]
    for h in range(heads):
        own = slice(h * count, (h + 1) * count)
        start = block + h * columns
        bias = came_ref[:, start : start + columns, :].astype(F32).reshape(count, count) * LOG2E
        own_lanes = jnp.where(lane == h, 1.0, 0.0).astype(BF16)
        for j in range(columns):
            scaled = dot(k_ref[j] * own_lanes, q_ref[j], 1, 1) * (size ** (-0.5) * LOG2E) + bias
            score_ref[j, own, :] = jnp.where(valid, scaled, -1000000000.0 * LOG2E)
    for h in range(heads):
        own = slice(h * count, (h + 1) * count)
        tops = [jnp.max(score_ref[j, own, :].reshape(-1, 8, count), axis=0) for j in range(columns)]
        tops = [jnp.max(top, axis=0, keepdims=True) for top in tops]
        for j in range(columns):
            expo_ref[j, own, :] = jnp.exp2(score_ref[j, own, :] - tops[j]).astype(BF16)
    for j in range(columns):
        for h in range(heads):
            own = slice(h * size, (h + 1) * size)
            output = dot(v_ref[j, h], expo_ref[j, h * count : (h + 1) * count, :], 1, 0)
            attended = gate_ref[j, own, :] * (output[:size] * (1.0 / output[size : size + 1]))
            attended_ref[j, own, :] = attended.astype(BF16)
    w_out = w_out_ref[...]
    for j in range(columns):
        added_ref[pl.ds(j, count, stride=columns), :] = dot(attended_ref[j], w_out, 0, 0)
    for p, d in enumerate(order):
        rows = slice(p * block, (p + 1) * block)
        result = (wide_ref[rows, :] + added_ref[rows, :]).reshape(-1, columns, w_out.shape[1])
        out_ref[d * columns : (d + 1) * columns] = result.astype(BF16)


def call(kernel, outs, operands, specs=None, scratch=()):
    size = sum(a.size * a.dtype.itemsize for a in list(operands) + list(outs))
    return pl.pallas_call(
        kernel,
        out_shape=[jax.ShapeDtypeStruct(o.shape, o.dtype) for o in outs],
        in_specs=[VMEM] * len(operands) if specs is None else specs,
        out_specs=[VMEM] * len(outs),
        scratch_shapes=list(scratch),
        cost_estimate=pl.CostEstimate(flops=0, bytes_accessed=size, transcendentals=0),
        compiler_params=pltpu.CompilerParams(vmem_limit_bytes=24 * 2**20),
    )(*operands)


def shape(dims, dtype):
    return jax.ShapeDtypeStruct(dims, dtype)


def exchange(x, order=None):
    groups = None if order is None else [order]
    return lax.all_to_all(x, "dap", split_axis=0, concat_axis=0, tiled=True, axis_index_groups=groups)


def kernel_body(pair, w_proj, w_gate_out, w_out, w_qkvg, w_bias, w_att_out, length):
    rows, count, channels = pair.shape
    hidden = w_out.shape[0]
    blocks = count // rows
    heads, width = w_bias.shape[1], w_att_out.shape[0]
    square = (rows, count, channels)
    wide = pltpu.VMEM((rows * count, channels), F32)

    sent, gate, w_rows = call(
        project_kernel,
        [shape((blocks, 16 * rows, count), BF16), shape(square, F32), shape((heads * rows, channels), F32)],
        [length] + [pltpu.with_memory_space_constraint(x, pltpu.HBM) for x in (pair, w_proj, w_gate_out, w_bias.T)],
        [SMEM] + [HBM] * 4,
        [
            pltpu.VMEM(pair.shape, BF16),
            pltpu.VMEM(w_proj.shape, BF16),
            pltpu.VMEM(w_gate_out.shape, BF16),
            pltpu.VMEM((heads, channels), BF16),
            pltpu.VMEM(square, BF16),
            pltpu.SemaphoreType.DMA((4,)),
        ],
    )
    came = exchange(sent, ORDER)
    (product,) = call(
        product_kernel,
        [shape((blocks, 8 * rows, count), BF16)],
        (came,),
        scratch=[pltpu.VMEM((blocks * 16 * rows, count), F32)],
    )
    came = exchange(product, ORDER)
    (sent,) = call(
        functools.partial(middle_kernel, ORDER),
        [shape((blocks, (8 + heads) * rows, count), BF16)],
        (came, gate, pair, w_out, w_rows),
        scratch=[wide, pltpu.VMEM(square, F32), pltpu.VMEM(square, BF16)],
    )
    came = exchange(sent, ORDER)
    (out,) = call(
        functools.partial(attention_kernel, ORDER, heads),
        [shape((count, rows, channels), BF16)],
        (length, came, w_qkvg, w_att_out),
        [SMEM] + [VMEM] * 3,
        [
            wide,
            wide,
            pltpu.VMEM(square, BF16),
            pltpu.VMEM((rows, count, width), BF16),
            pltpu.VMEM((rows, count, width), BF16),
            pltpu.VMEM((rows, heads, width // heads + 16, count), BF16),
            pltpu.VMEM((rows, width, count), F32),
            pltpu.VMEM((rows, heads * count, count), F32),
            pltpu.VMEM((rows, heads * count, count), BF16),
            pltpu.VMEM((rows, width, count), BF16),
        ],
    )
    return out


def matmul(spec, a, b):
    return jnp.einsum(spec, a, b, preferred_element_type=jnp.float32)


def whole_body(pair, w_proj, w_gate_out, w_out, w_qkvg, w_bias, w_att_out, length):
    row_count, full_count, channels = pair.shape
    hidden = w_out.shape[0]
    device_count = full_count // row_count
    share = hidden // device_count
    my_index = lax.axis_index("dap")
    positions = jnp.arange(full_count, dtype=jnp.int32)
    valid_keys = (positions < length[0]).astype(jnp.float32)
    row_valid = lax.dynamic_slice_in_dim(valid_keys, my_index * row_count, row_count)

    normed = layer_norm(pair.astype(jnp.float32), 2).astype(jnp.bfloat16)
    projected = matmul("rnc,ce->ern", normed, w_proj)
    pair_mask = row_valid[:, None] * valid_keys[None, :]
    left = jax.nn.sigmoid(projected[hidden : 2 * hidden]) * projected[:hidden] * pair_mask
    right = jax.nn.sigmoid(projected[3 * hidden :]) * projected[2 * hidden : 3 * hidden] * pair_mask
    blocks = (device_count, share * row_count, full_count)
    left = left.astype(jnp.bfloat16).reshape(blocks)
    right = right.astype(jnp.bfloat16).reshape(blocks)
    columns = jnp.transpose(
        pair.reshape(row_count, device_count, row_count, channels), (1, 0, 2, 3)
    )
    cut = share * row_count * full_count
    sent = jnp.concatenate(
        [
            left.reshape(device_count, cut),
            right.reshape(device_count, cut),
            columns.reshape(device_count, row_count * row_count * channels),
        ],
        axis=1,
    )
    came = exchange(sent.reshape(device_count, -1, channels)).reshape(device_count, -1)
    rows = (device_count, share, row_count, full_count)
    left = jnp.transpose(came[:, :cut].reshape(rows), (1, 0, 2, 3))
    right = jnp.transpose(came[:, cut : 2 * cut].reshape(rows), (1, 0, 2, 3))
    columns = came[:, 2 * cut :].reshape(full_count, row_count, channels)

    square = (share, full_count, full_count)
    product = matmul("cjk,cik->cji", right.reshape(square), left.reshape(square))
    product = product.astype(jnp.bfloat16).reshape(share, device_count, row_count, full_count)
    product = exchange(jnp.transpose(product, (1, 0, 2, 3)))
    product = product.reshape(hidden, row_count, full_count)
    product_norm = layer_norm(product.astype(jnp.float32), 0).astype(jnp.bfloat16)
    update = matmul("cji,cd->ijd", product_norm, w_out)
    normed = layer_norm(columns.astype(jnp.float32), 2).astype(jnp.bfloat16)
    gate_out = jax.nn.sigmoid(matmul("ijc,cd->ijd", normed, w_gate_out))
    columns = (columns.astype(jnp.float32) + gate_out * update).astype(jnp.bfloat16)

    normed_mid = layer_norm(columns.astype(jnp.float32), 2).astype(jnp.bfloat16)
    heads = w_bias.shape[1]
    width = w_att_out.shape[0]
    head_size = width // heads
    bias = matmul("kic,ch->hik", normed_mid, w_bias).astype(jnp.bfloat16)
    bias = exchange(jnp.broadcast_to(bias[None], (device_count,) + bias.shape))
    bias = jnp.transpose(bias, (1, 0, 2, 3)).reshape(heads, full_count, full_count)

    mixed = matmul("ijc,ce->ije", normed_mid, w_qkvg)
    per_head = (full_count, row_count, heads, head_size)
    queries = mixed[..., :width].astype(jnp.bfloat16).reshape(per_head)
    keys = mixed[..., width : 2 * width].astype(jnp.bfloat16).reshape(per_head)
    values = mixed[..., 2 * width : 3 * width].astype(jnp.bfloat16).reshape(per_head)
    gate = jax.nn.sigmoid(mixed[..., 3 * width :])
    score = matmul("ijhd,kjhd->jhik", queries, keys) * head_size ** (-0.5)
    score = score + bias.astype(jnp.float32)[None]
    score = jnp.where(valid_keys > 0, score, -1000000000.0)
    top = jnp.max(score, axis=3, keepdims=True)
    expo = jnp.exp(score - top)
    weights = (expo / jnp.sum(expo, axis=3, keepdims=True)).astype(jnp.bfloat16)
    output = matmul("jhik,kjhd->ijhd", weights, values)
    attended = (gate * output.reshape(full_count, row_count, width)).astype(jnp.bfloat16)
    result = columns.astype(jnp.float32) + matmul("ije,ec->ijc", attended, w_att_out)
    return result.astype(jnp.bfloat16)


def body(pair, w_proj, w_gate_out, w_out, w_qkvg, w_bias, w_att_out, length):
    rows, count, channels = pair.shape
    share = w_out.shape[0] * rows // count
    fits = share == rows == 8 and count // rows == len(ORDER) and count == channels == w_att_out.shape[0] == 128
    chosen = kernel_body if fits else whole_body
    return chosen(pair, w_proj, w_gate_out, w_out, w_qkvg, w_bias, w_att_out, length)


def solution(mesh):
    placed = (P(("rep", "dap"), None, None), P(), P(), P(), P(), P(), P(), P("rep"))
    return jax.shard_map(
        body, mesh=mesh, in_specs=placed, out_specs=P("rep", "dap", None), check_vma=False
    )
```

```python
import functools

import jax
import jax.numpy as jnp
from jax import lax
from jax.experimental import pallas as pl
from jax.experimental.pallas import tpu as pltpu
from jax.sharding import PartitionSpec as P

VMEM = pl.BlockSpec(memory_space=pltpu.VMEM)
SMEM = pl.BlockSpec(memory_space=pltpu.SMEM)
HBM = pl.BlockSpec(memory_space=pltpu.HBM)
BF16, F32 = jnp.bfloat16, jnp.float32
LOG2E = 1.4426950408889634
ORDERS = [
    [4, 0, 12, 8, 14, 10, 6, 2, 5, 1, 13, 9, 15, 11, 7, 3],
    [6, 10, 5, 2, 1, 11, 15, 3, 4, 8, 12, 0, 14, 7, 13, 9],
]


def dot(a, b, over_a, over_b):
    return lax.dot_general(a, b, (((over_a,), (over_b,)), ((), ())), preferred_element_type=F32)


def sigmoid(x):
    return 0.5 * jnp.tanh(0.5 * x) + 0.5


def layer_norm(x, axis):
    mean = jnp.mean(x, axis=axis, keepdims=True)
    centered = x - mean
    spread = jnp.mean(centered * centered, axis=axis, keepdims=True)
    return centered * lax.rsqrt(spread + 1e-05)


def devices(orders):
    first = lax.axis_index("rep") == 0
    return [jnp.where(first, jnp.int32(a), jnp.int32(b)) for a, b in zip(*orders)]


def interleave(a, b, blocks):
    split = (blocks, a.shape[0] // blocks, a.shape[1])
    return jnp.concatenate([a.reshape(split), b.reshape(split)], axis=1).astype(BF16)


def project_kernel(
    length_ref,
    pair_hbm,
    w_hbm,
    w_gate_hbm,
    w_bias_hbm,
    out_ref,
    gate_ref,
    w_rows_ref,
    pair_ref,
    w_ref,
    w_gate_ref,
    w_bias_ref,
    normed_ref,
    sems,
):
    rows, count, channels = pair_ref.shape
    blocks = out_ref.shape[0]
    hidden = w_ref.shape[1] // 4
    copies = [
        pltpu.make_async_copy(pair_hbm, pair_ref, sems.at[0]),
        pltpu.make_async_copy(w_hbm, w_ref, sems.at[1]),
        pltpu.make_async_copy(w_gate_hbm, w_gate_ref, sems.at[2]),
        pltpu.make_async_copy(w_bias_hbm, w_bias_ref, sems.at[3]),
    ]
    for copy in copies:
        copy.start()
    first_row = lax.axis_index("dap") * rows
    length = length_ref[0]
    key_valid = jnp.where(lax.broadcasted_iota(jnp.int32, (1, count), 1) < length, 1.0, 0.0)
    for copy in copies:
        copy.wait()
    for r in range(rows):
        normed_ref[r] = layer_norm(pair_ref[r].astype(F32), 1).astype(BF16)
    w_turned = w_ref[...].T
    for r in range(rows):
        projected = dot(w_turned, normed_ref[r], 1, 1)
        mask = key_valid * jnp.where(first_row + r < length, 1.0, 0.0)
        left = sigmoid(projected[hidden : 2 * hidden]) * projected[:hidden] * mask
        right = sigmoid(projected[3 * hidden :]) * projected[2 * hidden : 3 * hidden] * mask
        out_ref[:, 16 * r : 16 * r + 16, :] = interleave(left, right, blocks)
    w_gate = w_gate_ref[...]
    for r in range(rows):
        gate_ref[r] = sigmoid(dot(normed_ref[r], w_gate, 1, 0))
    w_bias = w_bias_ref[...].astype(F32)
    for h in range(w_bias.shape[0]):
        w_rows_ref[h * rows : (h + 1) * rows, :] = jnp.broadcast_to(w_bias[h : h + 1], (rows, channels))


def product_kernel(came_ref, out_ref, wide_ref):
    blocks, per_block, count = came_ref.shape
    for p in range(blocks):
        wide_ref[p * per_block : (p + 1) * per_block, :] = came_ref[p].astype(F32)

    def product(c):
        left = wide_ref[pl.ds(c, count, stride=16), :].astype(BF16)
        right = wide_ref[pl.ds(8 + c, count, stride=16), :].astype(BF16)
        return dot(left, right, 1, 1)

    for c in range(0, 8, 2):
        out_ref[:, 8 * c : 8 * c + 16, :] = interleave(product(c), product(c + 1), blocks)


def middle_kernel(orders, came_ref, gate_ref, pair_ref, w_out_ref, w_rows_ref, out_ref, wide_ref, mid_ref, normed_ref):
    rows, count, channels = pair_ref.shape
    starts = [pl.multiple_of(d * rows, rows) for d in devices(orders)]
    blocks, per_block, _ = came_ref.shape
    hidden = blocks * per_block // rows

    def load(p):
        return came_ref[p].astype(F32).reshape(per_block // rows, rows, count)

    mean = jnp.zeros((rows, count), F32)
    for p in range(blocks):
        mean += jnp.sum(load(p), axis=0)
    mean = mean * (1.0 / hidden)
    spread = jnp.zeros((rows, count), F32)
    for p in range(blocks):
        spread += jnp.sum(jnp.square(load(p) - mean), axis=0)
    scale = lax.rsqrt(spread * (1.0 / hidden) + 1e-05)
    for p in range(blocks):
        part = (load(p) - mean) * scale
        wide_ref[p * per_block : (p + 1) * per_block, :] = part.reshape(per_block, count)
    w_out = w_out_ref[...]
    for r in range(rows):
        mid_ref[r] = pair_ref[r].astype(F32)

    def by_block(r):
        return jnp.concatenate([mid_ref[r, pl.ds(start, rows), :] for start in starts], axis=0)

    for r in range(rows):
        product = wide_ref[pl.ds(r, hidden, stride=rows), :].astype(BF16)
        update = dot(product, w_out, 0, 0)
        gate = jnp.concatenate([gate_ref[r, pl.ds(start, rows), :] for start in starts], axis=0)
        mid_ref[r] = (by_block(r) + gate * update).astype(BF16).astype(F32)
    for r in range(0, rows, 2):
        out_ref[:, 8 * r : 8 * r + 16, :] = interleave(mid_ref[r], mid_ref[r + 1], blocks)
    for r in range(rows):
        normed_ref[r] = layer_norm(mid_ref[r], 1).astype(BF16)
    w_bias = w_rows_ref[...]
    own = lax.broadcasted_iota(jnp.int32, w_bias.shape, 0) % rows
    bias = jnp.zeros((w_bias.shape[0], count), F32)
    for r in range(rows):
        bias += dot(jnp.where(own == r, w_bias, 0.0).astype(BF16), normed_ref[r], 1, 1)
    out_ref[:, 8 * rows :, :] = jnp.broadcast_to(bias.astype(BF16)[None], (blocks,) + bias.shape)


def attention_kernel(
    orders,
    heads,
    length_ref,
    came_ref,
    w_ref,
    w_out_ref,
    out_ref,
    wide_ref,
    added_ref,
    normed_ref,
    q_ref,
    k_ref,
    v_ref,
    gate_ref,
    score_ref,
    expo_ref,
    attended_ref,
):
    columns, width, count = gate_ref.shape
    size = width // heads
    blocks, block = came_ref.shape[0], columns * columns
    for p in range(blocks):
        wide_ref[p * block : (p + 1) * block, :] = came_ref[p, :block].astype(F32)
    for j in range(columns):
        normed_ref[j] = layer_norm(wide_ref[pl.ds(j, count, stride=columns), :], 1).astype(BF16)
    w = w_ref[...]
    for j in range(columns):
        qk = dot(normed_ref[j], w[:, : 2 * width], 1, 0)
        q_ref[j] = qk[:, :width].astype(BF16)
        k_ref[j] = qk[:, width:].astype(BF16)
    w_turned = w[:, 2 * width :].T
    ones = jnp.where(lax.broadcasted_iota(jnp.int32, (16, count), 0) == 0, 1.0, 0.0).astype(BF16)
    for j in range(columns):
        vg = dot(w_turned, normed_ref[j], 1, 1)
        gate_ref[j] = sigmoid(vg[width:])
        for h in range(heads):
            v_ref[j, h, :size, :] = vg[h * size : (h + 1) * size].astype(BF16)
            v_ref[j, h, size:, :] = ones
    lane = lax.broadcasted_iota(jnp.int32, (count, width), 1) // size
    own_devices = devices(orders)
    within = lax.broadcasted_iota(jnp.int32, (columns, count), 0)
    token = jnp.concatenate([within + d * columns for d in own_devices], axis=0)
    valid = token < length_ref[0]
    for h in range(heads):
        own = slice(h * count, (h + 1) * count)
        start = block + h * columns
        bias = came_ref[:, start : start + columns, :].astype(F32).reshape(count, count) * LOG2E
        own_lanes = jnp.where(lane == h, 1.0, 0.0).astype(BF16)
        for j in range(columns):
            scaled = dot(k_ref[j] * own_lanes, q_ref[j], 1, 1) * (size ** (-0.5) * LOG2E) + bias
            score_ref[j, own, :] = jnp.where(valid, scaled, -1000000000.0 * LOG2E)
    for h in range(heads):
        own = slice(h * count, (h + 1) * count)
        tops = [jnp.max(score_ref[j, own, :].reshape(-1, 8, count), axis=0) for j in range(columns)]
        tops = [jnp.max(top, axis=0, keepdims=True) for top in tops]
        for j in range(columns):
            expo_ref[j, own, :] = jnp.exp2(score_ref[j, own, :] - tops[j]).astype(BF16)
    for j in range(columns):
        for h in range(heads):
            own = slice(h * size, (h + 1) * size)
            output = dot(v_ref[j, h], expo_ref[j, h * count : (h + 1) * count, :], 1, 0)
            attended = gate_ref[j, own, :] * (output[:size] * (1.0 / output[size : size + 1]))
            attended_ref[j, own, :] = attended.astype(BF16)
    w_out = w_out_ref[...]
    for j in range(columns):
        added_ref[pl.ds(j, count, stride=columns), :] = dot(attended_ref[j], w_out, 0, 0)
    for p, d in enumerate(own_devices):
        rows = slice(p * block, (p + 1) * block)
        result = (wide_ref[rows, :] + added_ref[rows, :]).reshape(-1, columns, w_out.shape[1])
        out_ref[pl.ds(pl.multiple_of(d * columns, columns), columns)] = result.astype(BF16)


def call(kernel, outs, operands, specs=None, scratch=()):
    size = sum(a.size * a.dtype.itemsize for a in list(operands) + list(outs))
    return pl.pallas_call(
        kernel,
        out_shape=[jax.ShapeDtypeStruct(o.shape, o.dtype) for o in outs],
        in_specs=[VMEM] * len(operands) if specs is None else specs,
        out_specs=[VMEM] * len(outs),
        scratch_shapes=list(scratch),
        cost_estimate=pl.CostEstimate(flops=0, bytes_accessed=size, transcendentals=0),
        compiler_params=pltpu.CompilerParams(vmem_limit_bytes=24 * 2**20),
    )(*operands)


def shape(dims, dtype):
    return jax.ShapeDtypeStruct(dims, dtype)


def exchange(x, orders=None):
    if orders is None:
        return lax.all_to_all(x, "dap", split_axis=0, concat_axis=0, tiled=True)
    groups = [[rep * len(order) + d for d in order] for rep, order in enumerate(orders)]
    return lax.all_to_all(x, ("rep", "dap"), split_axis=0, concat_axis=0, tiled=True, axis_index_groups=groups)


def kernel_body(pair, w_proj, w_gate_out, w_out, w_qkvg, w_bias, w_att_out, length):
    rows, count, channels = pair.shape
    hidden = w_out.shape[0]
    blocks = count // rows
    heads, width = w_bias.shape[1], w_att_out.shape[0]
    square = (rows, count, channels)
    wide = pltpu.VMEM((rows * count, channels), F32)

    sent, gate, w_rows = call(
        project_kernel,
        [shape((blocks, 16 * rows, count), BF16), shape(square, F32), shape((heads * rows, channels), F32)],
        [length] + [pltpu.with_memory_space_constraint(x, pltpu.HBM) for x in (pair, w_proj, w_gate_out, w_bias.T)],
        [SMEM] + [HBM] * 4,
        [
            pltpu.VMEM(pair.shape, BF16),
            pltpu.VMEM(w_proj.shape, BF16),
            pltpu.VMEM(w_gate_out.shape, BF16),
            pltpu.VMEM((heads, channels), BF16),
            pltpu.VMEM(square, BF16),
            pltpu.SemaphoreType.DMA((4,)),
        ],
    )
    came = exchange(sent, ORDERS)
    (product,) = call(
        product_kernel,
        [shape((blocks, 8 * rows, count), BF16)],
        (came,),
        scratch=[pltpu.VMEM((blocks * 16 * rows, count), F32)],
    )
    came = exchange(product, ORDERS)
    (sent,) = call(
        functools.partial(middle_kernel, ORDERS),
        [shape((blocks, (8 + heads) * rows, count), BF16)],
        (came, gate, pair, w_out, w_rows),
        scratch=[wide, pltpu.VMEM(square, F32), pltpu.VMEM(square, BF16)],
    )
    came = exchange(sent, ORDERS)
    (out,) = call(
        functools.partial(attention_kernel, ORDERS, heads),
        [shape((count, rows, channels), BF16)],
        (length, came, w_qkvg, w_att_out),
        [SMEM] + [VMEM] * 3,
        [
            wide,
            wide,
            pltpu.VMEM(square, BF16),
            pltpu.VMEM((rows, count, width), BF16),
            pltpu.VMEM((rows, count, width), BF16),
            pltpu.VMEM((rows, heads, width // heads + 16, count), BF16),
            pltpu.VMEM((rows, width, count), F32),
            pltpu.VMEM((rows, heads * count, count), F32),
            pltpu.VMEM((rows, heads * count, count), BF16),
            pltpu.VMEM((rows, width, count), BF16),
        ],
    )
    return out


def matmul(spec, a, b):
    return jnp.einsum(spec, a, b, preferred_element_type=jnp.float32)


def whole_body(pair, w_proj, w_gate_out, w_out, w_qkvg, w_bias, w_att_out, length):
    row_count, full_count, channels = pair.shape
    hidden = w_out.shape[0]
    device_count = full_count // row_count
    share = hidden // device_count
    my_index = lax.axis_index("dap")
    positions = jnp.arange(full_count, dtype=jnp.int32)
    valid_keys = (positions < length[0]).astype(jnp.float32)
    row_valid = lax.dynamic_slice_in_dim(valid_keys, my_index * row_count, row_count)

    normed = layer_norm(pair.astype(jnp.float32), 2).astype(jnp.bfloat16)
    projected = matmul("rnc,ce->ern", normed, w_proj)
    pair_mask = row_valid[:, None] * valid_keys[None, :]
    left = jax.nn.sigmoid(projected[hidden : 2 * hidden]) * projected[:hidden] * pair_mask
    right = jax.nn.sigmoid(projected[3 * hidden :]) * projected[2 * hidden : 3 * hidden] * pair_mask
    blocks = (device_count, share * row_count, full_count)
    left = left.astype(jnp.bfloat16).reshape(blocks)
    right = right.astype(jnp.bfloat16).reshape(blocks)
    columns = jnp.transpose(
        pair.reshape(row_count, device_count, row_count, channels), (1, 0, 2, 3)
    )
    cut = share * row_count * full_count
    sent = jnp.concatenate(
        [
            left.reshape(device_count, cut),
            right.reshape(device_count, cut),
            columns.reshape(device_count, row_count * row_count * channels),
        ],
        axis=1,
    )
    came = exchange(sent.reshape(device_count, -1, channels)).reshape(device_count, -1)
    rows = (device_count, share, row_count, full_count)
    left = jnp.transpose(came[:, :cut].reshape(rows), (1, 0, 2, 3))
    right = jnp.transpose(came[:, cut : 2 * cut].reshape(rows), (1, 0, 2, 3))
    columns = came[:, 2 * cut :].reshape(full_count, row_count, channels)

    square = (share, full_count, full_count)
    product = matmul("cjk,cik->cji", right.reshape(square), left.reshape(square))
    product = product.astype(jnp.bfloat16).reshape(share, device_count, row_count, full_count)
    product = exchange(jnp.transpose(product, (1, 0, 2, 3)))
    product = product.reshape(hidden, row_count, full_count)
    product_norm = layer_norm(product.astype(jnp.float32), 0).astype(jnp.bfloat16)
    update = matmul("cji,cd->ijd", product_norm, w_out)
    normed = layer_norm(columns.astype(jnp.float32), 2).astype(jnp.bfloat16)
    gate_out = jax.nn.sigmoid(matmul("ijc,cd->ijd", normed, w_gate_out))
    columns = (columns.astype(jnp.float32) + gate_out * update).astype(jnp.bfloat16)

    normed_mid = layer_norm(columns.astype(jnp.float32), 2).astype(jnp.bfloat16)
    heads = w_bias.shape[1]
    width = w_att_out.shape[0]
    head_size = width // heads
    bias = matmul("kic,ch->hik", normed_mid, w_bias).astype(jnp.bfloat16)
    bias = exchange(jnp.broadcast_to(bias[None], (device_count,) + bias.shape))
    bias = jnp.transpose(bias, (1, 0, 2, 3)).reshape(heads, full_count, full_count)

    mixed = matmul("ijc,ce->ije", normed_mid, w_qkvg)
    per_head = (full_count, row_count, heads, head_size)
    queries = mixed[..., :width].astype(jnp.bfloat16).reshape(per_head)
    keys = mixed[..., width : 2 * width].astype(jnp.bfloat16).reshape(per_head)
    values = mixed[..., 2 * width : 3 * width].astype(jnp.bfloat16).reshape(per_head)
    gate = jax.nn.sigmoid(mixed[..., 3 * width :])
    score = matmul("ijhd,kjhd->jhik", queries, keys) * head_size ** (-0.5)
    score = score + bias.astype(jnp.float32)[None]
    score = jnp.where(valid_keys > 0, score, -1000000000.0)
    top = jnp.max(score, axis=3, keepdims=True)
    expo = jnp.exp(score - top)
    weights = (expo / jnp.sum(expo, axis=3, keepdims=True)).astype(jnp.bfloat16)
    output = matmul("jhik,kjhd->ijhd", weights, values)
    attended = (gate * output.reshape(full_count, row_count, width)).astype(jnp.bfloat16)
    result = columns.astype(jnp.float32) + matmul("ije,ec->ijc", attended, w_att_out)
    return result.astype(jnp.bfloat16)


def body(pair, w_proj, w_gate_out, w_out, w_qkvg, w_bias, w_att_out, length):
    rows, count, channels = pair.shape
    share = w_out.shape[0] * rows // count
    fits = share == rows == 8 and count // rows == len(ORDERS[0]) and count == channels == w_att_out.shape[0] == 128
    chosen = kernel_body if fits else whole_body
    return chosen(pair, w_proj, w_gate_out, w_out, w_qkvg, w_bias, w_att_out, length)


def solution(mesh):
    placed = (P(("rep", "dap"), None, None), P(), P(), P(), P(), P(), P(), P("rep"))
    return jax.shard_map(
        body, mesh=mesh, in_specs=placed, out_specs=P("rep", "dap", None), check_vma=False
    )
```

```python
import functools

import jax
import jax.numpy as jnp
from jax import lax
from jax.experimental import pallas as pl
from jax.experimental.pallas import tpu as pltpu
from jax.sharding import PartitionSpec as P

VMEM = pl.BlockSpec(memory_space=pltpu.VMEM)
SMEM = pl.BlockSpec(memory_space=pltpu.SMEM)
HBM = pl.BlockSpec(memory_space=pltpu.HBM)
BF16, F32 = jnp.bfloat16, jnp.float32
ORDERS = [
    [4, 0, 12, 8, 14, 10, 6, 2, 5, 1, 13, 9, 15, 11, 7, 3],
    [6, 10, 5, 2, 1, 11, 15, 3, 4, 8, 12, 0, 14, 7, 13, 9],
]


def dot(a, b, over_a, over_b):
    return lax.dot_general(a, b, (((over_a,), (over_b,)), ((), ())), preferred_element_type=F32)


def sigmoid(x):
    return 0.5 * jnp.tanh(0.5 * x) + 0.5


def layer_norm(x, axis):
    mean = jnp.mean(x, axis=axis, keepdims=True)
    centered = x - mean
    spread = jnp.mean(centered * centered, axis=axis, keepdims=True)
    return centered * lax.rsqrt(spread + 1e-05)


def devices(orders):
    first = lax.axis_index("rep") == 0
    return [jnp.where(first, jnp.int32(a), jnp.int32(b)) for a, b in zip(*orders)]


def interleave(a, b, blocks):
    split = (blocks, a.shape[0] // blocks, a.shape[1])
    return jnp.concatenate([a.reshape(split), b.reshape(split)], axis=1).astype(BF16)


def project_kernel(
    length_ref,
    pair_hbm,
    w_hbm,
    w_gate_hbm,
    w_bias_hbm,
    out_ref,
    gate_ref,
    w_rows_ref,
    pair_ref,
    w_ref,
    w_gate_ref,
    w_bias_ref,
    normed_ref,
    sems,
):
    rows, count, channels = pair_ref.shape
    blocks = out_ref.shape[0]
    hidden = w_ref.shape[1] // 4
    parts = [pl.ds(start, rows // 2) for start in (0, rows // 2)]
    copies = [
        pltpu.make_async_copy(pair_hbm.at[parts[0]], pair_ref.at[parts[0]], sems.at[0]),
        pltpu.make_async_copy(pair_hbm.at[parts[1]], pair_ref.at[parts[1]], sems.at[1]),
        pltpu.make_async_copy(w_hbm, w_ref, sems.at[2]),
        pltpu.make_async_copy(w_gate_hbm, w_gate_ref, sems.at[3]),
        pltpu.make_async_copy(w_bias_hbm, w_bias_ref, sems.at[4]),
    ]
    for copy in copies:
        copy.start()
    first_row = lax.axis_index("dap") * rows
    length = length_ref[0]
    key_valid = jnp.where(lax.broadcasted_iota(jnp.int32, (1, count), 1) < length, 1.0, 0.0)
    for r in range(rows):
        if r % (rows // 2) == 0:
            copies[r // (rows // 2)].wait()
        normed_ref[r] = layer_norm(pair_ref[r].astype(F32), 1).astype(BF16)
    for copy in copies[2:]:
        copy.wait()
    w_turned = w_ref[...].T
    for r in range(rows):
        projected = dot(w_turned, normed_ref[r], 1, 1)
        mask = key_valid * jnp.where(first_row + r < length, 1.0, 0.0)
        left = sigmoid(projected[hidden : 2 * hidden]) * projected[:hidden] * mask
        right = sigmoid(projected[3 * hidden :]) * projected[2 * hidden : 3 * hidden] * mask
        out_ref[:, 16 * r : 16 * r + 16, :] = interleave(left, right, blocks)
    w_gate = w_gate_ref[...]
    for r in range(rows):
        gate_ref[r] = sigmoid(dot(normed_ref[r], w_gate, 1, 0))
    w_bias = w_bias_ref[...].astype(F32)
    for h in range(w_bias.shape[0]):
        w_rows_ref[h * rows : (h + 1) * rows, :] = jnp.broadcast_to(w_bias[h : h + 1], (rows, channels))


def product_kernel(came_ref, out_ref, wide_ref):
    blocks, per_block, count = came_ref.shape
    for p in range(blocks):
        wide_ref[p * per_block : (p + 1) * per_block, :] = came_ref[p].astype(F32)

    def product(c):
        left = wide_ref[pl.ds(c, count, stride=16), :].astype(BF16)
        right = wide_ref[pl.ds(8 + c, count, stride=16), :].astype(BF16)
        return dot(left, right, 1, 1)

    for c in range(0, 8, 2):
        out_ref[:, 8 * c : 8 * c + 16, :] = interleave(product(c), product(c + 1), blocks)


def middle_kernel(orders, came_ref, gate_ref, pair_ref, w_out_ref, w_rows_ref, out_ref, wide_ref, mid_ref, normed_ref):
    rows, count, channels = pair_ref.shape
    starts = [pl.multiple_of(d * rows, rows) for d in devices(orders)]
    blocks, per_block, _ = came_ref.shape
    hidden = blocks * per_block // rows

    def load(p):
        return came_ref[p].astype(F32).reshape(per_block // rows, rows, count)

    mean = jnp.zeros((rows, count), F32)
    for p in range(blocks):
        mean += jnp.sum(load(p), axis=0)
    mean = mean * (1.0 / hidden)
    spread = jnp.zeros((rows, count), F32)
    for p in range(blocks):
        spread += jnp.sum(jnp.square(load(p) - mean), axis=0)
    scale = lax.rsqrt(spread * (1.0 / hidden) + 1e-05)
    for p in range(blocks):
        part = (load(p) - mean) * scale
        wide_ref[p * per_block : (p + 1) * per_block, :] = part.reshape(per_block, count)
    w_out = w_out_ref[...]
    for r in range(rows):
        mid_ref[r] = pair_ref[r].astype(F32)

    def by_block(r):
        return jnp.concatenate([mid_ref[r, pl.ds(start, rows), :] for start in starts], axis=0)

    for r in range(rows):
        product = wide_ref[pl.ds(r, hidden, stride=rows), :].astype(BF16)
        update = dot(product, w_out, 0, 0)
        gate = jnp.concatenate([gate_ref[r, pl.ds(start, rows), :] for start in starts], axis=0)
        mid_ref[r] = (by_block(r) + gate * update).astype(BF16).astype(F32)
    for r in range(0, rows, 2):
        out_ref[:, 8 * r : 8 * r + 16, :] = interleave(mid_ref[r], mid_ref[r + 1], blocks)
    for r in range(rows):
        normed_ref[r] = layer_norm(mid_ref[r], 1).astype(BF16)
    w_bias = w_rows_ref[...]
    own = lax.broadcasted_iota(jnp.int32, w_bias.shape, 0) % rows
    bias = jnp.zeros((w_bias.shape[0], count), F32)
    for r in range(rows):
        bias += dot(jnp.where(own == r, w_bias, 0.0).astype(BF16), normed_ref[r], 1, 1)
    out_ref[:, 8 * rows :, :] = jnp.broadcast_to(bias.astype(BF16)[None], (blocks,) + bias.shape)


def attention_kernel(
    orders,
    heads,
    length_ref,
    came_ref,
    w_ref,
    w_out_ref,
    out_ref,
    wide_ref,
    added_ref,
    normed_ref,
    q_ref,
    k_ref,
    v_ref,
    gate_ref,
    score_ref,
    expo_ref,
    attended_ref,
):
    columns, width, count = gate_ref.shape
    size = width // heads
    blocks, block = came_ref.shape[0], columns * columns
    for p in range(blocks):
        wide_ref[p * block : (p + 1) * block, :] = came_ref[p, :block].astype(F32)
    for j in range(columns):
        normed_ref[j] = layer_norm(wide_ref[pl.ds(j, count, stride=columns), :], 1).astype(BF16)
    w = w_ref[...]
    for j in range(columns):
        qk = dot(normed_ref[j], w[:, : 2 * width], 1, 0)
        q_ref[j] = qk[:, :width].astype(BF16)
        k_ref[j] = qk[:, width:].astype(BF16)
    w_turned = w[:, 2 * width :].T
    ones = jnp.where(lax.broadcasted_iota(jnp.int32, (16, count), 0) == 0, 1.0, 0.0).astype(BF16)
    for j in range(columns):
        vg = dot(w_turned, normed_ref[j], 1, 1)
        gate_ref[j] = sigmoid(vg[width:])
        for h in range(heads):
            v_ref[j, h, :size, :] = vg[h * size : (h + 1) * size].astype(BF16)
            v_ref[j, h, size:, :] = ones
    lane = lax.broadcasted_iota(jnp.int32, (count, width), 1) // size
    own_devices = devices(orders)
    within = lax.broadcasted_iota(jnp.int32, (columns, count), 0)
    token = jnp.concatenate([within + d * columns for d in own_devices], axis=0)
    valid = token < length_ref[0]
    for h in range(heads):
        own = slice(h * count, (h + 1) * count)
        start = block + h * columns
        bias = came_ref[:, start : start + columns, :].astype(F32).reshape(count, count)
        own_lanes = jnp.where(lane == h, 1.0, 0.0).astype(BF16)
        for j in range(columns):
            scaled = dot(k_ref[j] * own_lanes, q_ref[j], 1, 1) * size ** (-0.5) + bias
            score_ref[j, own, :] = jnp.where(valid, scaled, -1000000000.0)
    for h in range(heads):
        own = slice(h * count, (h + 1) * count)
        tops = [jnp.max(score_ref[j, own, :].reshape(-1, 8, count), axis=0) for j in range(columns)]
        tops = [jnp.max(top, axis=0, keepdims=True) for top in tops]
        for j in range(columns):
            expo_ref[j, own, :] = jnp.exp(score_ref[j, own, :] - tops[j]).astype(BF16)
    for j in range(columns):
        for h in range(heads):
            own = slice(h * size, (h + 1) * size)
            output = dot(v_ref[j, h], expo_ref[j, h * count : (h + 1) * count, :], 1, 0)
            attended = gate_ref[j, own, :] * (output[:size] * (1.0 / output[size : size + 1]))
            attended_ref[j, own, :] = attended.astype(BF16)
    w_out = w_out_ref[...]
    for j in range(columns):
        added_ref[pl.ds(j, count, stride=columns), :] = dot(attended_ref[j], w_out, 0, 0)
    for p, d in enumerate(own_devices):
        rows = slice(p * block, (p + 1) * block)
        result = (wide_ref[rows, :] + added_ref[rows, :]).reshape(-1, columns, w_out.shape[1])
        out_ref[pl.ds(pl.multiple_of(d * columns, columns), columns)] = result.astype(BF16)


def call(kernel, outs, operands, specs=None, scratch=()):
    size = sum(a.size * a.dtype.itemsize for a in list(operands) + list(outs))
    return pl.pallas_call(
        kernel,
        out_shape=[jax.ShapeDtypeStruct(o.shape, o.dtype) for o in outs],
        in_specs=[VMEM] * len(operands) if specs is None else specs,
        out_specs=[VMEM] * len(outs),
        scratch_shapes=list(scratch),
        cost_estimate=pl.CostEstimate(flops=0, bytes_accessed=size, transcendentals=0),
        compiler_params=pltpu.CompilerParams(vmem_limit_bytes=24 * 2**20),
    )(*operands)


def shape(dims, dtype):
    return jax.ShapeDtypeStruct(dims, dtype)


def exchange(x, orders=None):
    if orders is None:
        return lax.all_to_all(x, "dap", split_axis=0, concat_axis=0, tiled=True)
    groups = [[rep * len(order) + d for d in order] for rep, order in enumerate(orders)]
    return lax.all_to_all(x, ("rep", "dap"), split_axis=0, concat_axis=0, tiled=True, axis_index_groups=groups)


def kernel_body(pair, w_proj, w_gate_out, w_out, w_qkvg, w_bias, w_att_out, length):
    rows, count, channels = pair.shape
    hidden = w_out.shape[0]
    blocks = count // rows
    heads, width = w_bias.shape[1], w_att_out.shape[0]
    square = (rows, count, channels)
    wide = pltpu.VMEM((rows * count, channels), F32)

    sent, gate, w_rows = call(
        project_kernel,
        [shape((blocks, 16 * rows, count), BF16), shape(square, F32), shape((heads * rows, channels), F32)],
        [length] + [pltpu.with_memory_space_constraint(x, pltpu.HBM) for x in (pair, w_proj, w_gate_out, w_bias.T)],
        [SMEM] + [HBM] * 4,
        [
            pltpu.VMEM(pair.shape, BF16),
            pltpu.VMEM(w_proj.shape, BF16),
            pltpu.VMEM(w_gate_out.shape, BF16),
            pltpu.VMEM((heads, channels), BF16),
            pltpu.VMEM(square, BF16),
            pltpu.SemaphoreType.DMA((5,)),
        ],
    )
    came = exchange(sent, ORDERS)
    (product,) = call(
        product_kernel,
        [shape((blocks, 8 * rows, count), BF16)],
        (came,),
        scratch=[pltpu.VMEM((blocks * 16 * rows, count), F32)],
    )
    came = exchange(product, ORDERS)
    (sent,) = call(
        functools.partial(middle_kernel, ORDERS),
        [shape((blocks, (8 + heads) * rows, count), BF16)],
        (came, gate, pair, w_out, w_rows),
        scratch=[wide, pltpu.VMEM(square, F32), pltpu.VMEM(square, BF16)],
    )
    came = exchange(sent, ORDERS)
    (out,) = call(
        functools.partial(attention_kernel, ORDERS, heads),
        [shape((count, rows, channels), BF16)],
        (length, came, w_qkvg, w_att_out),
        [SMEM] + [VMEM] * 3,
        [
            wide,
            wide,
            pltpu.VMEM(square, BF16),
            pltpu.VMEM((rows, count, width), BF16),
            pltpu.VMEM((rows, count, width), BF16),
            pltpu.VMEM((rows, heads, width // heads + 16, count), BF16),
            pltpu.VMEM((rows, width, count), F32),
            pltpu.VMEM((rows, heads * count, count), F32),
            pltpu.VMEM((rows, heads * count, count), BF16),
            pltpu.VMEM((rows, width, count), BF16),
        ],
    )
    return out


def matmul(spec, a, b):
    return jnp.einsum(spec, a, b, preferred_element_type=jnp.float32)


def whole_body(pair, w_proj, w_gate_out, w_out, w_qkvg, w_bias, w_att_out, length):
    row_count, full_count, channels = pair.shape
    hidden = w_out.shape[0]
    device_count = full_count // row_count
    share = hidden // device_count
    my_index = lax.axis_index("dap")
    positions = jnp.arange(full_count, dtype=jnp.int32)
    valid_keys = (positions < length[0]).astype(jnp.float32)
    row_valid = lax.dynamic_slice_in_dim(valid_keys, my_index * row_count, row_count)

    normed = layer_norm(pair.astype(jnp.float32), 2).astype(jnp.bfloat16)
    projected = matmul("rnc,ce->ern", normed, w_proj)
    pair_mask = row_valid[:, None] * valid_keys[None, :]
    left = jax.nn.sigmoid(projected[hidden : 2 * hidden]) * projected[:hidden] * pair_mask
    right = jax.nn.sigmoid(projected[3 * hidden :]) * projected[2 * hidden : 3 * hidden] * pair_mask
    blocks = (device_count, share * row_count, full_count)
    left = left.astype(jnp.bfloat16).reshape(blocks)
    right = right.astype(jnp.bfloat16).reshape(blocks)
    columns = jnp.transpose(
        pair.reshape(row_count, device_count, row_count, channels), (1, 0, 2, 3)
    )
    cut = share * row_count * full_count
    sent = jnp.concatenate(
        [
            left.reshape(device_count, cut),
            right.reshape(device_count, cut),
            columns.reshape(device_count, row_count * row_count * channels),
        ],
        axis=1,
    )
    came = exchange(sent.reshape(device_count, -1, channels)).reshape(device_count, -1)
    rows = (device_count, share, row_count, full_count)
    left = jnp.transpose(came[:, :cut].reshape(rows), (1, 0, 2, 3))
    right = jnp.transpose(came[:, cut : 2 * cut].reshape(rows), (1, 0, 2, 3))
    columns = came[:, 2 * cut :].reshape(full_count, row_count, channels)

    square = (share, full_count, full_count)
    product = matmul("cjk,cik->cji", right.reshape(square), left.reshape(square))
    product = product.astype(jnp.bfloat16).reshape(share, device_count, row_count, full_count)
    product = exchange(jnp.transpose(product, (1, 0, 2, 3)))
    product = product.reshape(hidden, row_count, full_count)
    product_norm = layer_norm(product.astype(jnp.float32), 0).astype(jnp.bfloat16)
    update = matmul("cji,cd->ijd", product_norm, w_out)
    normed = layer_norm(columns.astype(jnp.float32), 2).astype(jnp.bfloat16)
    gate_out = jax.nn.sigmoid(matmul("ijc,cd->ijd", normed, w_gate_out))
    columns = (columns.astype(jnp.float32) + gate_out * update).astype(jnp.bfloat16)

    normed_mid = layer_norm(columns.astype(jnp.float32), 2).astype(jnp.bfloat16)
    heads = w_bias.shape[1]
    width = w_att_out.shape[0]
    head_size = width // heads
    bias = matmul("kic,ch->hik", normed_mid, w_bias).astype(jnp.bfloat16)
    bias = exchange(jnp.broadcast_to(bias[None], (device_count,) + bias.shape))
    bias = jnp.transpose(bias, (1, 0, 2, 3)).reshape(heads, full_count, full_count)

    mixed = matmul("ijc,ce->ije", normed_mid, w_qkvg)
    per_head = (full_count, row_count, heads, head_size)
    queries = mixed[..., :width].astype(jnp.bfloat16).reshape(per_head)
    keys = mixed[..., width : 2 * width].astype(jnp.bfloat16).reshape(per_head)
    values = mixed[..., 2 * width : 3 * width].astype(jnp.bfloat16).reshape(per_head)
    gate = jax.nn.sigmoid(mixed[..., 3 * width :])
    score = matmul("ijhd,kjhd->jhik", queries, keys) * head_size ** (-0.5)
    score = score + bias.astype(jnp.float32)[None]
    score = jnp.where(valid_keys > 0, score, -1000000000.0)
    top = jnp.max(score, axis=3, keepdims=True)
    expo = jnp.exp(score - top)
    weights = (expo / jnp.sum(expo, axis=3, keepdims=True)).astype(jnp.bfloat16)
    output = matmul("jhik,kjhd->ijhd", weights, values)
    attended = (gate * output.reshape(full_count, row_count, width)).astype(jnp.bfloat16)
    result = columns.astype(jnp.float32) + matmul("ije,ec->ijc", attended, w_att_out)
    return result.astype(jnp.bfloat16)


def body(pair, w_proj, w_gate_out, w_out, w_qkvg, w_bias, w_att_out, length):
    rows, count, channels = pair.shape
    share = w_out.shape[0] * rows // count
    fits = share == rows == 8 and count // rows == len(ORDERS[0]) and count == channels == w_att_out.shape[0] == 128
    chosen = kernel_body if fits else whole_body
    return chosen(pair, w_proj, w_gate_out, w_out, w_qkvg, w_bias, w_att_out, length)


def solution(mesh):
    placed = (P(("rep", "dap"), None, None), P(), P(), P(), P(), P(), P(), P("rep"))
    return jax.shard_map(
        body, mesh=mesh, in_specs=placed, out_specs=P("rep", "dap", None), check_vma=False
    )
```

```python
import functools

import jax
import jax.numpy as jnp
from jax import lax
from jax.experimental import pallas as pl
from jax.experimental.pallas import tpu as pltpu
from jax.sharding import PartitionSpec as P

VMEM = pl.BlockSpec(memory_space=pltpu.VMEM)
SMEM = pl.BlockSpec(memory_space=pltpu.SMEM)
HBM = pl.BlockSpec(memory_space=pltpu.HBM)
BF16, F32 = jnp.bfloat16, jnp.float32
ORDER = [6, 10, 2, 14, 9, 5, 13, 1, 3, 11, 7, 15, 0, 12, 8, 4]


def dot(a, b, over_a, over_b):
    return lax.dot_general(a, b, (((over_a,), (over_b,)), ((), ())), preferred_element_type=F32)


def sigmoid(x):
    return 0.5 * jnp.tanh(0.5 * x) + 0.5


def layer_norm(x, axis):
    mean = jnp.mean(x, axis=axis, keepdims=True)
    centered = x - mean
    spread = jnp.mean(centered * centered, axis=axis, keepdims=True)
    return centered * lax.rsqrt(spread + 1e-05)


def by_block(x, order):
    size = x.shape[0] // len(order)
    return jnp.concatenate([x[d * size : (d + 1) * size] for d in order], axis=0)


def interleave(a, b, blocks):
    split = (blocks, a.shape[0] // blocks, a.shape[1])
    return jnp.concatenate([a.reshape(split), b.reshape(split)], axis=1).astype(BF16)


def project_kernel(
    length_ref,
    pair_hbm,
    w_hbm,
    w_gate_hbm,
    w_bias_hbm,
    out_ref,
    gate_ref,
    w_rows_ref,
    pair_ref,
    w_ref,
    w_gate_ref,
    w_bias_ref,
    normed_ref,
    sems,
):
    rows, count, channels = pair_ref.shape
    blocks = out_ref.shape[0]
    hidden = w_ref.shape[1] // 4
    parts = [pl.ds(start, rows // 2) for start in (0, rows // 2)]
    copies = [
        pltpu.make_async_copy(pair_hbm.at[parts[0]], pair_ref.at[parts[0]], sems.at[0]),
        pltpu.make_async_copy(pair_hbm.at[parts[1]], pair_ref.at[parts[1]], sems.at[1]),
        pltpu.make_async_copy(w_hbm, w_ref, sems.at[2]),
        pltpu.make_async_copy(w_gate_hbm, w_gate_ref, sems.at[3]),
        pltpu.make_async_copy(w_bias_hbm, w_bias_ref, sems.at[4]),
    ]
    for copy in copies:
        copy.start()
    first_row = lax.axis_index("dap") * rows
    length = length_ref[0]
    key_valid = jnp.where(lax.broadcasted_iota(jnp.int32, (1, count), 1) < length, 1.0, 0.0)
    for r in range(rows):
        if r % (rows // 2) == 0:
            copies[r // (rows // 2)].wait()
        normed_ref[r] = layer_norm(pair_ref[r].astype(F32), 1).astype(BF16)
    for copy in copies[2:]:
        copy.wait()
    w_turned = w_ref[...].T
    for r in range(rows):
        projected = dot(w_turned, normed_ref[r], 1, 1)
        mask = key_valid * jnp.where(first_row + r < length, 1.0, 0.0)
        left = sigmoid(projected[hidden : 2 * hidden]) * projected[:hidden] * mask
        right = sigmoid(projected[3 * hidden :]) * projected[2 * hidden : 3 * hidden] * mask
        out_ref[:, 16 * r : 16 * r + 16, :] = interleave(left, right, blocks)
    w_gate = w_gate_ref[...]
    for r in range(rows):
        gate_ref[r] = sigmoid(dot(normed_ref[r], w_gate, 1, 0))
    w_bias = w_bias_ref[...].astype(F32)
    for h in range(w_bias.shape[0]):
        w_rows_ref[h * rows : (h + 1) * rows, :] = jnp.broadcast_to(w_bias[h : h + 1], (rows, channels))


def product_kernel(came_ref, out_ref, wide_ref):
    blocks, per_block, count = came_ref.shape
    for p in range(blocks):
        wide_ref[p * per_block : (p + 1) * per_block, :] = came_ref[p].astype(F32)

    def product(c):
        left = wide_ref[pl.ds(c, count, stride=16), :].astype(BF16)
        right = wide_ref[pl.ds(8 + c, count, stride=16), :].astype(BF16)
        return dot(left, right, 1, 1)

    for c in range(0, 8, 2):
        out_ref[:, 8 * c : 8 * c + 16, :] = interleave(product(c), product(c + 1), blocks)


def middle_kernel(order, came_ref, gate_ref, pair_ref, w_out_ref, w_rows_ref, out_ref, wide_ref, mid_ref, normed_ref):
    rows, count, channels = pair_ref.shape
    blocks, per_block, _ = came_ref.shape
    hidden = blocks * per_block // rows

    def load(p):
        return came_ref[p].astype(F32).reshape(per_block // rows, rows, count)

    mean = jnp.zeros((rows, count), F32)
    for p in range(blocks):
        mean += jnp.sum(load(p), axis=0)
    mean = mean * (1.0 / hidden)
    spread = jnp.zeros((rows, count), F32)
    for p in range(blocks):
        spread += jnp.sum(jnp.square(load(p) - mean), axis=0)
    scale = lax.rsqrt(spread * (1.0 / hidden) + 1e-05)
    for p in range(blocks):
        part = (load(p) - mean) * scale
        wide_ref[p * per_block : (p + 1) * per_block, :] = part.reshape(per_block, count)
    w_out = w_out_ref[...]
    for r in range(rows):
        product = wide_ref[pl.ds(r, hidden, stride=rows), :].astype(BF16)
        update = dot(product, w_out, 0, 0)
        pair, gate = by_block(pair_ref[r].astype(F32), order), by_block(gate_ref[r], order)
        mid = (pair + gate * update).astype(BF16)
        mid_ref[r] = mid.astype(F32)
    for r in range(0, rows, 2):
        out_ref[:, 8 * r : 8 * r + 16, :] = interleave(mid_ref[r], mid_ref[r + 1], blocks)
    for r in range(rows):
        normed_ref[r] = layer_norm(mid_ref[r], 1).astype(BF16)
    w_bias = w_rows_ref[...]
    own = lax.broadcasted_iota(jnp.int32, w_bias.shape, 0) % rows
    bias = jnp.zeros((w_bias.shape[0], count), F32)
    for r in range(rows):
        bias += dot(jnp.where(own == r, w_bias, 0.0).astype(BF16), normed_ref[r], 1, 1)
    out_ref[:, 8 * rows :, :] = jnp.broadcast_to(bias.astype(BF16)[None], (blocks,) + bias.shape)


def attention_kernel(
    order,
    heads,
    length_ref,
    came_ref,
    w_ref,
    w_out_ref,
    out_ref,
    wide_ref,
    added_ref,
    normed_ref,
    q_ref,
    k_ref,
    v_ref,
    gate_ref,
    score_ref,
    expo_ref,
    attended_ref,
):
    columns, width, count = gate_ref.shape
    size = width // heads
    blocks, block = came_ref.shape[0], columns * columns
    for p in range(blocks):
        wide_ref[p * block : (p + 1) * block, :] = came_ref[p, :block].astype(F32)
    for j in range(columns):
        normed_ref[j] = layer_norm(wide_ref[pl.ds(j, count, stride=columns), :], 1).astype(BF16)
    w = w_ref[...]
    for j in range(columns):
        qk = dot(normed_ref[j], w[:, : 2 * width], 1, 0)
        q_ref[j] = qk[:, :width].astype(BF16)
        k_ref[j] = qk[:, width:].astype(BF16)
    w_turned = w[:, 2 * width :].T
    ones = jnp.where(lax.broadcasted_iota(jnp.int32, (16, count), 0) == 0, 1.0, 0.0).astype(BF16)
    for j in range(columns):
        vg = dot(w_turned, normed_ref[j], 1, 1)
        gate_ref[j] = sigmoid(vg[width:])
        for h in range(heads):
            v_ref[j, h, :size, :] = vg[h * size : (h + 1) * size].astype(BF16)
            v_ref[j, h, size:, :] = ones
    lane = lax.broadcasted_iota(jnp.int32, (count, width), 1) // size
    token = by_block(lax.broadcasted_iota(jnp.int32, (count, count), 0), order)
    valid = token < length_ref[0]
    for h in range(heads):
        own = slice(h * count, (h + 1) * count)
        start = block + h * columns
        bias = came_ref[:, start : start + columns, :].astype(F32).reshape(count, count)
        own_lanes = jnp.where(lane == h, 1.0, 0.0).astype(BF16)
        for j in range(columns):
            scaled = dot(k_ref[j] * own_lanes, q_ref[j], 1, 1) * size ** (-0.5) + bias
            score_ref[j, own, :] = jnp.where(valid, scaled, -1000000000.0)
    for h in range(heads):
        own = slice(h * count, (h + 1) * count)
        tops = [jnp.max(score_ref[j, own, :].reshape(-1, 8, count), axis=0) for j in range(columns)]
        tops = [jnp.max(top, axis=0, keepdims=True) for top in tops]
        for j in range(columns):
            expo_ref[j, own, :] = jnp.exp(score_ref[j, own, :] - tops[j]).astype(BF16)
    for j in range(columns):
        for h in range(heads):
            own = slice(h * size, (h + 1) * size)
            output = dot(v_ref[j, h], expo_ref[j, h * count : (h + 1) * count, :], 1, 0)
            attended = gate_ref[j, own, :] * (output[:size] * (1.0 / output[size : size + 1]))
            attended_ref[j, own, :] = attended.astype(BF16)
    w_out = w_out_ref[...]
    for j in range(columns):
        added_ref[pl.ds(j, count, stride=columns), :] = dot(attended_ref[j], w_out, 0, 0)
    for p, d in enumerate(order):
        rows = slice(p * block, (p + 1) * block)
        result = (wide_ref[rows, :] + added_ref[rows, :]).reshape(-1, columns, w_out.shape[1])
        out_ref[d * columns : (d + 1) * columns] = result.astype(BF16)


def call(kernel, outs, operands, specs=None, scratch=()):
    size = sum(a.size * a.dtype.itemsize for a in list(operands) + list(outs))
    return pl.pallas_call(
        kernel,
        out_shape=[jax.ShapeDtypeStruct(o.shape, o.dtype) for o in outs],
        in_specs=[VMEM] * len(operands) if specs is None else specs,
        out_specs=[VMEM] * len(outs),
        scratch_shapes=list(scratch),
        cost_estimate=pl.CostEstimate(flops=0, bytes_accessed=size, transcendentals=0),
        compiler_params=pltpu.CompilerParams(vmem_limit_bytes=24 * 2**20),
    )(*operands)


def shape(dims, dtype):
    return jax.ShapeDtypeStruct(dims, dtype)


def exchange(x, order=None):
    groups = None if order is None else [order]
    return lax.all_to_all(x, "dap", split_axis=0, concat_axis=0, tiled=True, axis_index_groups=groups)


def kernel_body(pair, w_proj, w_gate_out, w_out, w_qkvg, w_bias, w_att_out, length):
    rows, count, channels = pair.shape
    hidden = w_out.shape[0]
    blocks = count // rows
    heads, width = w_bias.shape[1], w_att_out.shape[0]
    square = (rows, count, channels)
    wide = pltpu.VMEM((rows * count, channels), F32)

    sent, gate, w_rows = call(
        project_kernel,
        [shape((blocks, 16 * rows, count), BF16), shape(square, F32), shape((heads * rows, channels), F32)],
        [length] + [pltpu.with_memory_space_constraint(x, pltpu.HBM) for x in (pair, w_proj, w_gate_out, w_bias.T)],
        [SMEM] + [HBM] * 4,
        [
            pltpu.VMEM(pair.shape, BF16),
            pltpu.VMEM(w_proj.shape, BF16),
            pltpu.VMEM(w_gate_out.shape, BF16),
            pltpu.VMEM((heads, channels), BF16),
            pltpu.VMEM(square, BF16),
            pltpu.SemaphoreType.DMA((5,)),
        ],
    )
    came = exchange(sent, ORDER)
    (product,) = call(
        product_kernel,
        [shape((blocks, 8 * rows, count), BF16)],
        (came,),
        scratch=[pltpu.VMEM((blocks * 16 * rows, count), F32)],
    )
    came = exchange(product, ORDER)
    (sent,) = call(
        functools.partial(middle_kernel, ORDER),
        [shape((blocks, (8 + heads) * rows, count), BF16)],
        (came, gate, pair, w_out, w_rows),
        scratch=[wide, pltpu.VMEM(square, F32), pltpu.VMEM(square, BF16)],
    )
    came = exchange(sent, ORDER)
    (out,) = call(
        functools.partial(attention_kernel, ORDER, heads),
        [shape((count, rows, channels), BF16)],
        (length, came, w_qkvg, w_att_out),
        [SMEM] + [VMEM] * 3,
        [
            wide,
            wide,
            pltpu.VMEM(square, BF16),
            pltpu.VMEM((rows, count, width), BF16),
            pltpu.VMEM((rows, count, width), BF16),
            pltpu.VMEM((rows, heads, width // heads + 16, count), BF16),
            pltpu.VMEM((rows, width, count), F32),
            pltpu.VMEM((rows, heads * count, count), F32),
            pltpu.VMEM((rows, heads * count, count), BF16),
            pltpu.VMEM((rows, width, count), BF16),
        ],
    )
    return out


def matmul(spec, a, b):
    return jnp.einsum(spec, a, b, preferred_element_type=jnp.float32)


def whole_body(pair, w_proj, w_gate_out, w_out, w_qkvg, w_bias, w_att_out, length):
    row_count, full_count, channels = pair.shape
    hidden = w_out.shape[0]
    device_count = full_count // row_count
    share = hidden // device_count
    my_index = lax.axis_index("dap")
    positions = jnp.arange(full_count, dtype=jnp.int32)
    valid_keys = (positions < length[0]).astype(jnp.float32)
    row_valid = lax.dynamic_slice_in_dim(valid_keys, my_index * row_count, row_count)

    normed = layer_norm(pair.astype(jnp.float32), 2).astype(jnp.bfloat16)
    projected = matmul("rnc,ce->ern", normed, w_proj)
    pair_mask = row_valid[:, None] * valid_keys[None, :]
    left = jax.nn.sigmoid(projected[hidden : 2 * hidden]) * projected[:hidden] * pair_mask
    right = jax.nn.sigmoid(projected[3 * hidden :]) * projected[2 * hidden : 3 * hidden] * pair_mask
    blocks = (device_count, share * row_count, full_count)
    left = left.astype(jnp.bfloat16).reshape(blocks)
    right = right.astype(jnp.bfloat16).reshape(blocks)
    columns = jnp.transpose(
        pair.reshape(row_count, device_count, row_count, channels), (1, 0, 2, 3)
    )
    cut = share * row_count * full_count
    sent = jnp.concatenate(
        [
            left.reshape(device_count, cut),
            right.reshape(device_count, cut),
            columns.reshape(device_count, row_count * row_count * channels),
        ],
        axis=1,
    )
    came = exchange(sent.reshape(device_count, -1, channels)).reshape(device_count, -1)
    rows = (device_count, share, row_count, full_count)
    left = jnp.transpose(came[:, :cut].reshape(rows), (1, 0, 2, 3))
    right = jnp.transpose(came[:, cut : 2 * cut].reshape(rows), (1, 0, 2, 3))
    columns = came[:, 2 * cut :].reshape(full_count, row_count, channels)

    square = (share, full_count, full_count)
    product = matmul("cjk,cik->cji", right.reshape(square), left.reshape(square))
    product = product.astype(jnp.bfloat16).reshape(share, device_count, row_count, full_count)
    product = exchange(jnp.transpose(product, (1, 0, 2, 3)))
    product = product.reshape(hidden, row_count, full_count)
    product_norm = layer_norm(product.astype(jnp.float32), 0).astype(jnp.bfloat16)
    update = matmul("cji,cd->ijd", product_norm, w_out)
    normed = layer_norm(columns.astype(jnp.float32), 2).astype(jnp.bfloat16)
    gate_out = jax.nn.sigmoid(matmul("ijc,cd->ijd", normed, w_gate_out))
    columns = (columns.astype(jnp.float32) + gate_out * update).astype(jnp.bfloat16)

    normed_mid = layer_norm(columns.astype(jnp.float32), 2).astype(jnp.bfloat16)
    heads = w_bias.shape[1]
    width = w_att_out.shape[0]
    head_size = width // heads
    bias = matmul("kic,ch->hik", normed_mid, w_bias).astype(jnp.bfloat16)
    bias = exchange(jnp.broadcast_to(bias[None], (device_count,) + bias.shape))
    bias = jnp.transpose(bias, (1, 0, 2, 3)).reshape(heads, full_count, full_count)

    mixed = matmul("ijc,ce->ije", normed_mid, w_qkvg)
    per_head = (full_count, row_count, heads, head_size)
    queries = mixed[..., :width].astype(jnp.bfloat16).reshape(per_head)
    keys = mixed[..., width : 2 * width].astype(jnp.bfloat16).reshape(per_head)
    values = mixed[..., 2 * width : 3 * width].astype(jnp.bfloat16).reshape(per_head)
    gate = jax.nn.sigmoid(mixed[..., 3 * width :])
    score = matmul("ijhd,kjhd->jhik", queries, keys) * head_size ** (-0.5)
    score = score + bias.astype(jnp.float32)[None]
    score = jnp.where(valid_keys > 0, score, -1000000000.0)
    top = jnp.max(score, axis=3, keepdims=True)
    expo = jnp.exp(score - top)
    weights = (expo / jnp.sum(expo, axis=3, keepdims=True)).astype(jnp.bfloat16)
    output = matmul("jhik,kjhd->ijhd", weights, values)
    attended = (gate * output.reshape(full_count, row_count, width)).astype(jnp.bfloat16)
    result = columns.astype(jnp.float32) + matmul("ije,ec->ijc", attended, w_att_out)
    return result.astype(jnp.bfloat16)


def body(pair, w_proj, w_gate_out, w_out, w_qkvg, w_bias, w_att_out, length):
    rows, count, channels = pair.shape
    share = w_out.shape[0] * rows // count
    fits = share == rows == 8 and count // rows == len(ORDER) and count == channels == w_att_out.shape[0] == 128
    chosen = kernel_body if fits else whole_body
    return chosen(pair, w_proj, w_gate_out, w_out, w_qkvg, w_bias, w_att_out, length)


def solution(mesh):
    placed = (P(("rep", "dap"), None, None), P(), P(), P(), P(), P(), P(), P("rep"))
    return jax.shard_map(
        body, mesh=mesh, in_specs=placed, out_specs=P("rep", "dap", None), check_vma=False
    )
```

```python
import functools

import jax
import jax.numpy as jnp
from jax import lax
from jax.experimental import pallas as pl
from jax.experimental.pallas import tpu as pltpu
from jax.sharding import PartitionSpec as P

VMEM = pl.BlockSpec(memory_space=pltpu.VMEM)
SMEM = pl.BlockSpec(memory_space=pltpu.SMEM)
HBM = pl.BlockSpec(memory_space=pltpu.HBM)
BF16, F32 = jnp.bfloat16, jnp.float32
ORDER = [11, 10, 3, 14, 0, 2, 13, 1, 9, 12, 8, 4, 5, 6, 7, 15]


def dot(a, b, over_a, over_b):
    return lax.dot_general(a, b, (((over_a,), (over_b,)), ((), ())), preferred_element_type=F32)


def sigmoid(x):
    return 0.5 * jnp.tanh(0.5 * x) + 0.5


def layer_norm(x, axis):
    mean = jnp.mean(x, axis=axis, keepdims=True)
    centered = x - mean
    spread = jnp.mean(centered * centered, axis=axis, keepdims=True)
    return centered * lax.rsqrt(spread + 1e-05)


def by_block(x, order):
    size = x.shape[0] // len(order)
    return jnp.concatenate([x[d * size : (d + 1) * size] for d in order], axis=0)


def interleave(a, b, blocks):
    split = (blocks, a.shape[0] // blocks, a.shape[1])
    return jnp.concatenate([a.reshape(split), b.reshape(split)], axis=1).astype(BF16)


def project_kernel(
    length_ref,
    pair_hbm,
    w_hbm,
    w_gate_hbm,
    w_bias_hbm,
    out_ref,
    gate_ref,
    w_rows_ref,
    pair_ref,
    w_ref,
    w_gate_ref,
    w_bias_ref,
    normed_ref,
    sems,
):
    rows, count, channels = pair_ref.shape
    blocks = out_ref.shape[0]
    hidden = w_ref.shape[1] // 4
    parts = [pl.ds(start, rows // 2) for start in (0, rows // 2)]
    copies = [
        pltpu.make_async_copy(pair_hbm.at[parts[0]], pair_ref.at[parts[0]], sems.at[0]),
        pltpu.make_async_copy(pair_hbm.at[parts[1]], pair_ref.at[parts[1]], sems.at[1]),
        pltpu.make_async_copy(w_hbm, w_ref, sems.at[2]),
        pltpu.make_async_copy(w_gate_hbm, w_gate_ref, sems.at[3]),
        pltpu.make_async_copy(w_bias_hbm, w_bias_ref, sems.at[4]),
    ]
    for copy in copies:
        copy.start()
    first_row = lax.axis_index("dap") * rows
    length = length_ref[0]
    key_valid = jnp.where(lax.broadcasted_iota(jnp.int32, (1, count), 1) < length, 1.0, 0.0)
    for r in range(rows):
        if r % (rows // 2) == 0:
            copies[r // (rows // 2)].wait()
        normed_ref[r] = layer_norm(pair_ref[r].astype(F32), 1).astype(BF16)
    for copy in copies[2:]:
        copy.wait()
    w_turned = w_ref[...].T
    for r in range(rows):
        projected = dot(w_turned, normed_ref[r], 1, 1)
        mask = key_valid * jnp.where(first_row + r < length, 1.0, 0.0)
        left = sigmoid(projected[hidden : 2 * hidden]) * projected[:hidden] * mask
        right = sigmoid(projected[3 * hidden :]) * projected[2 * hidden : 3 * hidden] * mask
        out_ref[:, 16 * r : 16 * r + 16, :] = interleave(left, right, blocks)
    w_gate = w_gate_ref[...]
    for r in range(rows):
        gate_ref[r] = sigmoid(dot(normed_ref[r], w_gate, 1, 0))
    w_bias = w_bias_ref[...].astype(F32)
    for h in range(w_bias.shape[0]):
        w_rows_ref[h * rows : (h + 1) * rows, :] = jnp.broadcast_to(w_bias[h : h + 1], (rows, channels))


def product_kernel(came_ref, out_ref, wide_ref):
    blocks, per_block, count = came_ref.shape
    for p in range(blocks):
        wide_ref[p * per_block : (p + 1) * per_block, :] = came_ref[p].astype(F32)

    def product(c):
        left = wide_ref[pl.ds(c, count, stride=16), :].astype(BF16)
        right = wide_ref[pl.ds(8 + c, count, stride=16), :].astype(BF16)
        return dot(left, right, 1, 1)

    for c in range(0, 8, 2):
        out_ref[:, 8 * c : 8 * c + 16, :] = interleave(product(c), product(c + 1), blocks)


def middle_kernel(order, came_ref, gate_ref, pair_ref, w_out_ref, w_rows_ref, out_ref, wide_ref, mid_ref, normed_ref):
    rows, count, channels = pair_ref.shape
    blocks, per_block, _ = came_ref.shape
    hidden = blocks * per_block // rows

    def load(p):
        return came_ref[p].astype(F32).reshape(per_block // rows, rows, count)

    mean = jnp.zeros((rows, count), F32)
    for p in range(blocks):
        mean += jnp.sum(load(p), axis=0)
    mean = mean * (1.0 / hidden)
    spread = jnp.zeros((rows, count), F32)
    for p in range(blocks):
        spread += jnp.sum(jnp.square(load(p) - mean), axis=0)
    scale = lax.rsqrt(spread * (1.0 / hidden) + 1e-05)
    for p in range(blocks):
        part = (load(p) - mean) * scale
        wide_ref[p * per_block : (p + 1) * per_block, :] = part.reshape(per_block, count)
    w_out = w_out_ref[...]
    for r in range(rows):
        product = wide_ref[pl.ds(r, hidden, stride=rows), :].astype(BF16)
        update = dot(product, w_out, 0, 0)
        pair, gate = by_block(pair_ref[r].astype(F32), order), by_block(gate_ref[r], order)
        mid = (pair + gate * update).astype(BF16)
        mid_ref[r] = mid.astype(F32)
    for r in range(0, rows, 2):
        out_ref[:, 8 * r : 8 * r + 16, :] = interleave(mid_ref[r], mid_ref[r + 1], blocks)
    for r in range(rows):
        normed_ref[r] = layer_norm(mid_ref[r], 1).astype(BF16)
    w_bias = w_rows_ref[...]
    own = lax.broadcasted_iota(jnp.int32, w_bias.shape, 0) % rows
    bias = jnp.zeros((w_bias.shape[0], count), F32)
    for r in range(rows):
        bias += dot(jnp.where(own == r, w_bias, 0.0).astype(BF16), normed_ref[r], 1, 1)
    out_ref[:, 8 * rows :, :] = jnp.broadcast_to(bias.astype(BF16)[None], (blocks,) + bias.shape)


def attention_kernel(
    order,
    heads,
    length_ref,
    came_ref,
    w_ref,
    w_out_ref,
    out_ref,
    wide_ref,
    added_ref,
    normed_ref,
    q_ref,
    k_ref,
    v_ref,
    gate_ref,
    score_ref,
    expo_ref,
    attended_ref,
):
    columns, width, count = gate_ref.shape
    size = width // heads
    blocks, block = came_ref.shape[0], columns * columns
    for p in range(blocks):
        wide_ref[p * block : (p + 1) * block, :] = came_ref[p, :block].astype(F32)
    for j in range(columns):
        normed_ref[j] = layer_norm(wide_ref[pl.ds(j, count, stride=columns), :], 1).astype(BF16)
    w = w_ref[...]
    for j in range(columns):
        qk = dot(normed_ref[j], w[:, : 2 * width], 1, 0)
        q_ref[j] = qk[:, :width].astype(BF16)
        k_ref[j] = qk[:, width:].astype(BF16)
    w_turned = w[:, 2 * width :].T
    ones = jnp.where(lax.broadcasted_iota(jnp.int32, (16, count), 0) == 0, 1.0, 0.0).astype(BF16)
    for j in range(columns):
        vg = dot(w_turned, normed_ref[j], 1, 1)
        gate_ref[j] = sigmoid(vg[width:])
        for h in range(heads):
            v_ref[j, h, :size, :] = vg[h * size : (h + 1) * size].astype(BF16)
            v_ref[j, h, size:, :] = ones
    lane = lax.broadcasted_iota(jnp.int32, (count, width), 1) // size
    token = by_block(lax.broadcasted_iota(jnp.int32, (count, count), 0), order)
    valid = token < length_ref[0]
    for h in range(heads):
        own = slice(h * count, (h + 1) * count)
        start = block + h * columns
        bias = came_ref[:, start : start + columns, :].astype(F32).reshape(count, count)
        own_lanes = jnp.where(lane == h, 1.0, 0.0).astype(BF16)
        for j in range(columns):
            scaled = dot(k_ref[j] * own_lanes, q_ref[j], 1, 1) * size ** (-0.5) + bias
            score_ref[j, own, :] = jnp.where(valid, scaled, -1000000000.0)
    for h in range(heads):
        own = slice(h * count, (h + 1) * count)
        tops = [jnp.max(score_ref[j, own, :].reshape(-1, 8, count), axis=0) for j in range(columns)]
        tops = [jnp.max(top, axis=0, keepdims=True) for top in tops]
        for j in range(columns):
            expo_ref[j, own, :] = jnp.exp(score_ref[j, own, :] - tops[j]).astype(BF16)
    for j in range(columns):
        for h in range(heads):
            own = slice(h * size, (h + 1) * size)
            output = dot(v_ref[j, h], expo_ref[j, h * count : (h + 1) * count, :], 1, 0)
            attended = gate_ref[j, own, :] * (output[:size] * (1.0 / output[size : size + 1]))
            attended_ref[j, own, :] = attended.astype(BF16)
    w_out = w_out_ref[...]
    for j in range(columns):
        added_ref[pl.ds(j, count, stride=columns), :] = dot(attended_ref[j], w_out, 0, 0)
    for p, d in enumerate(order):
        rows = slice(p * block, (p + 1) * block)
        result = (wide_ref[rows, :] + added_ref[rows, :]).reshape(-1, columns, w_out.shape[1])
        out_ref[d * columns : (d + 1) * columns] = result.astype(BF16)


def call(kernel, outs, operands, specs=None, scratch=()):
    size = sum(a.size * a.dtype.itemsize for a in list(operands) + list(outs))
    return pl.pallas_call(
        kernel,
        out_shape=[jax.ShapeDtypeStruct(o.shape, o.dtype) for o in outs],
        in_specs=[VMEM] * len(operands) if specs is None else specs,
        out_specs=[VMEM] * len(outs),
        scratch_shapes=list(scratch),
        cost_estimate=pl.CostEstimate(flops=0, bytes_accessed=size, transcendentals=0),
        compiler_params=pltpu.CompilerParams(vmem_limit_bytes=24 * 2**20),
    )(*operands)


def shape(dims, dtype):
    return jax.ShapeDtypeStruct(dims, dtype)


def exchange(x, order=None):
    groups = None if order is None else [order]
    return lax.all_to_all(x, "dap", split_axis=0, concat_axis=0, tiled=True, axis_index_groups=groups)


def kernel_body(pair, w_proj, w_gate_out, w_out, w_qkvg, w_bias, w_att_out, length):
    rows, count, channels = pair.shape
    hidden = w_out.shape[0]
    blocks = count // rows
    heads, width = w_bias.shape[1], w_att_out.shape[0]
    square = (rows, count, channels)
    wide = pltpu.VMEM((rows * count, channels), F32)

    sent, gate, w_rows = call(
        project_kernel,
        [shape((blocks, 16 * rows, count), BF16), shape(square, F32), shape((heads * rows, channels), F32)],
        [length] + [pltpu.with_memory_space_constraint(x, pltpu.HBM) for x in (pair, w_proj, w_gate_out, w_bias.T)],
        [SMEM] + [HBM] * 4,
        [
            pltpu.VMEM(pair.shape, BF16),
            pltpu.VMEM(w_proj.shape, BF16),
            pltpu.VMEM(w_gate_out.shape, BF16),
            pltpu.VMEM((heads, channels), BF16),
            pltpu.VMEM(square, BF16),
            pltpu.SemaphoreType.DMA((5,)),
        ],
    )
    came = exchange(sent, ORDER)
    (product,) = call(
        product_kernel,
        [shape((blocks, 8 * rows, count), BF16)],
        (came,),
        scratch=[pltpu.VMEM((blocks * 16 * rows, count), F32)],
    )
    came = exchange(product, ORDER)
    (sent,) = call(
        functools.partial(middle_kernel, ORDER),
        [shape((blocks, (8 + heads) * rows, count), BF16)],
        (came, gate, pair, w_out, w_rows),
        scratch=[wide, pltpu.VMEM(square, F32), pltpu.VMEM(square, BF16)],
    )
    came = exchange(sent, ORDER)
    (out,) = call(
        functools.partial(attention_kernel, ORDER, heads),
        [shape((count, rows, channels), BF16)],
        (length, came, w_qkvg, w_att_out),
        [SMEM] + [VMEM] * 3,
        [
            wide,
            wide,
            pltpu.VMEM(square, BF16),
            pltpu.VMEM((rows, count, width), BF16),
            pltpu.VMEM((rows, count, width), BF16),
            pltpu.VMEM((rows, heads, width // heads + 16, count), BF16),
            pltpu.VMEM((rows, width, count), F32),
            pltpu.VMEM((rows, heads * count, count), F32),
            pltpu.VMEM((rows, heads * count, count), BF16),
            pltpu.VMEM((rows, width, count), BF16),
        ],
    )
    return out


def matmul(spec, a, b):
    return jnp.einsum(spec, a, b, preferred_element_type=jnp.float32)


def whole_body(pair, w_proj, w_gate_out, w_out, w_qkvg, w_bias, w_att_out, length):
    row_count, full_count, channels = pair.shape
    hidden = w_out.shape[0]
    device_count = full_count // row_count
    share = hidden // device_count
    my_index = lax.axis_index("dap")
    positions = jnp.arange(full_count, dtype=jnp.int32)
    valid_keys = (positions < length[0]).astype(jnp.float32)
    row_valid = lax.dynamic_slice_in_dim(valid_keys, my_index * row_count, row_count)

    normed = layer_norm(pair.astype(jnp.float32), 2).astype(jnp.bfloat16)
    projected = matmul("rnc,ce->ern", normed, w_proj)
    pair_mask = row_valid[:, None] * valid_keys[None, :]
    left = jax.nn.sigmoid(projected[hidden : 2 * hidden]) * projected[:hidden] * pair_mask
    right = jax.nn.sigmoid(projected[3 * hidden :]) * projected[2 * hidden : 3 * hidden] * pair_mask
    blocks = (device_count, share * row_count, full_count)
    left = left.astype(jnp.bfloat16).reshape(blocks)
    right = right.astype(jnp.bfloat16).reshape(blocks)
    columns = jnp.transpose(
        pair.reshape(row_count, device_count, row_count, channels), (1, 0, 2, 3)
    )
    cut = share * row_count * full_count
    sent = jnp.concatenate(
        [
            left.reshape(device_count, cut),
            right.reshape(device_count, cut),
            columns.reshape(device_count, row_count * row_count * channels),
        ],
        axis=1,
    )
    came = exchange(sent.reshape(device_count, -1, channels)).reshape(device_count, -1)
    rows = (device_count, share, row_count, full_count)
    left = jnp.transpose(came[:, :cut].reshape(rows), (1, 0, 2, 3))
    right = jnp.transpose(came[:, cut : 2 * cut].reshape(rows), (1, 0, 2, 3))
    columns = came[:, 2 * cut :].reshape(full_count, row_count, channels)

    square = (share, full_count, full_count)
    product = matmul("cjk,cik->cji", right.reshape(square), left.reshape(square))
    product = product.astype(jnp.bfloat16).reshape(share, device_count, row_count, full_count)
    product = exchange(jnp.transpose(product, (1, 0, 2, 3)))
    product = product.reshape(hidden, row_count, full_count)
    product_norm = layer_norm(product.astype(jnp.float32), 0).astype(jnp.bfloat16)
    update = matmul("cji,cd->ijd", product_norm, w_out)
    normed = layer_norm(columns.astype(jnp.float32), 2).astype(jnp.bfloat16)
    gate_out = jax.nn.sigmoid(matmul("ijc,cd->ijd", normed, w_gate_out))
    columns = (columns.astype(jnp.float32) + gate_out * update).astype(jnp.bfloat16)

    normed_mid = layer_norm(columns.astype(jnp.float32), 2).astype(jnp.bfloat16)
    heads = w_bias.shape[1]
    width = w_att_out.shape[0]
    head_size = width // heads
    bias = matmul("kic,ch->hik", normed_mid, w_bias).astype(jnp.bfloat16)
    bias = exchange(jnp.broadcast_to(bias[None], (device_count,) + bias.shape))
    bias = jnp.transpose(bias, (1, 0, 2, 3)).reshape(heads, full_count, full_count)

    mixed = matmul("ijc,ce->ije", normed_mid, w_qkvg)
    per_head = (full_count, row_count, heads, head_size)
    queries = mixed[..., :width].astype(jnp.bfloat16).reshape(per_head)
    keys = mixed[..., width : 2 * width].astype(jnp.bfloat16).reshape(per_head)
    values = mixed[..., 2 * width : 3 * width].astype(jnp.bfloat16).reshape(per_head)
    gate = jax.nn.sigmoid(mixed[..., 3 * width :])
    score = matmul("ijhd,kjhd->jhik", queries, keys) * head_size ** (-0.5)
    score = score + bias.astype(jnp.float32)[None]
    score = jnp.where(valid_keys > 0, score, -1000000000.0)
    top = jnp.max(score, axis=3, keepdims=True)
    expo = jnp.exp(score - top)
    weights = (expo / jnp.sum(expo, axis=3, keepdims=True)).astype(jnp.bfloat16)
    output = matmul("jhik,kjhd->ijhd", weights, values)
    attended = (gate * output.reshape(full_count, row_count, width)).astype(jnp.bfloat16)
    result = columns.astype(jnp.float32) + matmul("ije,ec->ijc", attended, w_att_out)
    return result.astype(jnp.bfloat16)


def body(pair, w_proj, w_gate_out, w_out, w_qkvg, w_bias, w_att_out, length):
    rows, count, channels = pair.shape
    share = w_out.shape[0] * rows // count
    fits = share == rows == 8 and count // rows == len(ORDER) and count == channels == w_att_out.shape[0] == 128
    chosen = kernel_body if fits else whole_body
    return chosen(pair, w_proj, w_gate_out, w_out, w_qkvg, w_bias, w_att_out, length)


def solution(mesh):
    placed = (P(("rep", "dap"), None, None), P(), P(), P(), P(), P(), P(), P("rep"))
    return jax.shard_map(
        body, mesh=mesh, in_specs=placed, out_specs=P("rep", "dap", None), check_vma=False
    )
```
